512 devices in a mesh: visit: 128 (over z, x_hi, y), quad: 4 (over x_lo, core).
Axes of the slice: x: 4 (x_hi: 2, x_lo: 2; x = x_hi * 2 + x_lo), y: 8, z: 8, core: 2. Of those that a mesh axis runs over, the one named last changes fastest.
Arguments:
- science: float32 [256, 192, 1024], P('visit', 'quad'), may hold values from -80 to 80
- reference_tiles: float32 [256, 192, 1024], P('visit', 'quad'), may hold values from -20 to 20
- visit_tiles: int32 [256, 2], P('visit'), may hold values from 0 to 255, as said below
- offsets: int32 [256], P('visit'), may hold values from 1 to 1023
- basis_rows: float32 [31, 31], replicated, may hold values from -1 to 2
- basis_cols: float32 [31, 31], replicated, may hold values from -1 to 2
Outputs:
- difference: float32 [256, 192, 1024], P('visit', 'quad')
- coadd_tiles: float32 [256, 192, 1024], P('visit', 'quad')
The draws below stay inside these ranges and needn't reach their ends.
Inputs may be any that keep to these rules, and one draw needn't show every extreme that they name: `visit_tiles`: tile t belongs to device t // 2 of visit and visit v to device v // 2; each of a visit's two tiles lies on a device at most 3 steps away, counted cyclically, and in every draw some visit's left tile is 3 steps ahead and some visit's right tile 3 steps behind. A visit's two tiles differ.
All inputs are finite; a program needn't handle non-finite values.
Results may differ from the reference program's by a relative error of at most 0.0003.
Values sent between devices are 32-bit elements; how exact they have to be, the bound alone decides.
A program may use at most 64 MiB of HBM per device.

```python
import jax
import jax.numpy as jnp
from jax import lax

COLS = 1024
NB = 31
KW = 31
REACH = 3
VISIT_DEV = 2
TILES_DEV = 2
VISITS = 256
TILES = 256
NY = 192


def pairing(key):
    devices = VISITS // VISIT_DEV
    keys = jax.random.split(jax.random.fold_in(key, 11), 7)
    home = jnp.arange(VISITS, dtype=jnp.int32) // VISIT_DEV
    step_first = jax.random.randint(keys[0], (VISITS,), -REACH, REACH + 1) * jax.random.randint(keys[1], (VISITS,), 0, 2)
    step_second = jax.random.randint(keys[2], (VISITS,), -REACH, REACH + 1) * jax.random.randint(keys[3], (VISITS,), 0, 2)
    step_first = step_first.at[0].set(REACH)
    step_second = step_second.at[1].set(-REACH)
    slot_first = jax.random.randint(keys[4], (VISITS,), 0, TILES_DEV)
    slot_second = jax.random.randint(keys[5], (VISITS,), 0, TILES_DEV)
    tile_first = (home + step_first) % devices * TILES_DEV + slot_first
    owner_second = (home + step_second) % devices
    tile_second = owner_second * TILES_DEV + slot_second
    tile_second = jnp.where(tile_second == tile_first, owner_second * TILES_DEV + (slot_second + 1) % TILES_DEV, tile_second)
    column_offsets = jax.random.randint(keys[6], (VISITS,), 1, COLS)
    column_offsets = column_offsets.at[0].set(COLS - 1).at[1].set(1)
    return (jnp.stack([tile_first, tile_second], axis=1).astype(jnp.int32), column_offsets.astype(jnp.int32))


def sky_tiles(key):
    base = jnp.clip(jax.random.normal(jax.random.fold_in(key, 12), (TILES, NY, COLS), jnp.float32), -5.0, 5.0)
    return base


def draw_visit_tiles(key, part):
    return pairing(key)[0]


def draw_offsets(key, part):
    return pairing(key)[1]


def draw_reference_tiles(key, part):
    tiles = sky_tiles(key)
    return tiles


def draw_science(key, part):
    tile_pairs, column_offsets = pairing(key)
    tiles = sky_tiles(key)
    key = jax.random.fold_in(key, 21)
    joined = jnp.concatenate([tiles[tile_pairs[:, 0]], tiles[tile_pairs[:, 1]]], axis=2)
    templates = jax.vmap(lambda row_image, shift_col: lax.dynamic_slice_in_dim(row_image, shift_col, COLS, 1))(joined, column_offsets)
    slopes = jax.random.uniform(jax.random.fold_in(key, 1), (VISITS,), jnp.float32, 1.5, 2.5)
    signs = 2.0 * jax.random.randint(jax.random.fold_in(key, 2), (VISITS,), 0, 2).astype(jnp.float32) - 1.0
    heights = jnp.arange(NY, dtype=jnp.float32) / NY - 0.5
    ramps = jnp.exp((slopes * signs)[:, None] * heights[None, :])[:, :, None]
    noise = 0.5 * jnp.clip(jax.random.normal(jax.random.fold_in(key, 3), (VISITS, NY, COLS), jnp.float32), -5.0, 5.0)
    return ramps * templates + noise


def draw_basis_rows(key, part):
    key = jax.random.fold_in(key, 31)
    values = jnp.clip(jax.random.normal(key, (NB, KW), jnp.float32), -4.0, 4.0) * KW ** (-0.5)
    centre = (jnp.arange(KW) == KW // 2).astype(jnp.float32)
    return values + centre[None, :]


def draw_basis_cols(key, part):
    key = jax.random.fold_in(key, 32)
    values = jnp.clip(jax.random.normal(key, (NB, KW), jnp.float32), -4.0, 4.0) * KW ** (-0.5)
    centre = (jnp.arange(KW) == KW // 2).astype(jnp.float32)
    return values + centre[None, :]


def setup_inputs(seed: int = 0) -> dict:
    arg_keys = jax.random.split(jax.random.key(seed), 7)
    return {
        "science": draw_science(jax.random.fold_in(arg_keys[6], 71), 0),
        "reference_tiles": draw_reference_tiles(jax.random.fold_in(arg_keys[6], 71), 0),
        "visit_tiles": draw_visit_tiles(jax.random.fold_in(arg_keys[6], 71), 0),
        "offsets": draw_offsets(jax.random.fold_in(arg_keys[6], 71), 0),
        "basis_rows": draw_basis_rows(jax.random.fold_in(arg_keys[6], 71), 0),
        "basis_cols": draw_basis_cols(jax.random.fold_in(arg_keys[6], 71), 0),
    }


def basis_images(template, basis_rows, basis_cols):
    half_width = KW // 2
    height = template.shape[0]
    col_count = template.shape[1]
    padded = jnp.pad(template, ((half_width, half_width), (half_width, half_width)))
    shifted = jnp.stack([padded[:, shift_col:shift_col + col_count] for shift_col in range(KW)])
    along_cols = jnp.einsum('bu,uyx->byx', basis_cols, shifted, precision=lax.Precision.HIGHEST)
    images = jnp.zeros((NB, height, col_count), jnp.float32)
    for shift_row in range(KW):
        images = images + basis_rows[:, shift_row, None, None] * along_cols[:, shift_row:shift_row + height, :]
    return images

def reference(science, reference_tiles, visit_tiles, offsets, basis_rows, basis_cols):
    pixels = NY * COLS

    def one_visit(inputs):
        tile_pair, offset, image = inputs
        joined = jnp.concatenate([reference_tiles[tile_pair[0]], reference_tiles[tile_pair[1]]], axis=1)
        template = lax.dynamic_slice_in_dim(joined, offset, COLS, 1)
        images = basis_images(template, basis_rows, basis_cols)
        flattened = images.reshape(NB, NY * COLS)
        normal = jnp.dot(flattened, flattened.T, precision=lax.Precision.HIGHEST) / pixels
        normal = normal + 0.01 * jnp.eye(NB, dtype=jnp.float32)
        moments = jnp.dot(flattened, image.reshape(NY * COLS), precision=lax.Precision.HIGHEST) / pixels
        factor = jnp.linalg.cholesky(normal)
        coefficients = jax.scipy.linalg.cho_solve((factor, True), moments)
        matched = jnp.einsum('b,byx->yx', coefficients, images, precision=lax.Precision.HIGHEST)
        diff_image = image - matched
        placed = lax.dynamic_update_slice(jnp.zeros((NY, 2 * COLS), jnp.float32), diff_image, (jnp.int32(0), offset.astype(jnp.int32)))
        return (diff_image, placed[:, :COLS], placed[:, COLS:])
    difference, left_parts, right_parts = lax.map(one_visit, (visit_tiles, offsets, science))
    coadd_tiles = jnp.zeros((TILES, NY, COLS), jnp.float32)
    coadd_tiles = coadd_tiles.at[visit_tiles[:, 0]].add(left_parts)
    coadd_tiles = coadd_tiles.at[visit_tiles[:, 1]].add(right_parts)
    return (difference, coadd_tiles)
```

```python
import functools

import jax
import jax.numpy as jnp
from jax import lax
from jax.experimental import pallas as pl
from jax.experimental.pallas import tpu as pltpu
from jax.sharding import PartitionSpec as P

MESH = pl.DeviceIdType.MESH
REACH = 3
LANES = 128
HALO = 16
EXT = 80
HIGHEST = lax.Precision.HIGHEST
F32 = jnp.float32
BF16 = jnp.bfloat16
SIGN = (1, -1)


def split(x):
    high = x.astype(BF16)
    return high, (x - high.astype(F32)).astype(BF16)


def kernel(
    pixels,
    sci, tiles, pairs, offs, brow, bcol,
    diff, coadd,
    metas, t1, snd2, r2, r3, pre, halo, tst, rmat, base, bmat, yhi, ylo, img,
    gacc, gbuf, cs, dt, dbank,
    ms, mr, s1, v1, s2, v2, s3, v3, hs, hr, gs, gr, ds_, dr,
):
    slots, rows, cols = sci.shape
    taps = 31
    count = 31
    half = rows // 2
    nv, nq = lax.axis_size("visit"), lax.axis_size("quad")
    me, q = lax.axis_index("visit"), lax.axis_index("quad")
    blocks = cols // LANES
    groups = half // 8

    def at_visit(step):
        return lax.rem(me + step + nv, nv)

    def at_quad(step):
        return lax.rem(q + step, nq)

    def remote(src, dst, send, recv, device):
        return pltpu.make_async_remote_copy(
            src_ref=src, dst_ref=dst, send_sem=send, recv_sem=recv,
            device_id=device, device_id_type=MESH,
        )

    steps = [step * sign for step in range(1, REACH + 1) for sign in SIGN]
    barrier = pltpu.get_barrier_semaphore()
    for step in steps:
        pl.semaphore_signal(barrier, inc=1, device_id={"visit": at_visit(step)}, device_id_type=MESH)
    for step in range(1, nq):
        pl.semaphore_signal(barrier, inc=1, device_id={"quad": at_quad(step)}, device_id_type=MESH)

    line = lax.broadcasted_iota(jnp.int32, (8, LANES), 0)
    own = jnp.zeros((8, LANES), jnp.int32)
    for slot in range(slots):
        for place, value in enumerate((pairs[slot, 0], pairs[slot, 1], offs[slot])):
            own = jnp.where(line == 3 * slot + place, value, own)
    metas[REACH] = own
    pl.semaphore_wait(barrier, len(steps) + nq - 1)

    meta_copies = [
        remote(metas.at[REACH], metas.at[REACH - step], ms.at[REACH - step], mr.at[REACH - step],
               {"visit": at_visit(step)})
        for step in steps
    ]
    for copy in meta_copies:
        copy.start()
    ahead = [{"visit": at_visit(sign)} for sign in SIGN]
    hop1 = [
        remote(tiles.at[t], t1.at[d, t], s1.at[d, t], v1.at[d, t], ahead[d])
        for t in range(slots) for d in range(2)
    ]
    for copy in hop1:
        copy.start()

    tst[...] = jnp.zeros_like(tst)
    bmat[...] = jnp.zeros_like(bmat)
    blank = jnp.zeros((32, LANES), F32)
    row_high = brow[...].astype(BF16).astype(F32)
    row_low = brow[...] - row_high
    wide_high = jnp.concatenate([row_high, blank], axis=1)
    wide_low = jnp.concatenate([row_low, blank], axis=1)
    base[0] = (
        pltpu.roll(wide_high, 1, 1) + pltpu.roll(wide_low, EXT + 1, 1) + pltpu.roll(wide_high, 2 * EXT + 1, 1)
    )
    col_high = bcol[...].astype(BF16).astype(F32)
    back = 2 * LANES - (taps - 1)
    base[1] = pltpu.roll(jnp.concatenate([col_high, blank], axis=1), back, 1)
    base[2] = pltpu.roll(jnp.concatenate([bcol[...] - col_high, blank], axis=1), back, 1)

    @pl.loop(0, count)
    def _(k):
        first = pl.multiple_of(k * rows, 16)
        line_k = jnp.broadcast_to(base[0, pl.ds(k, 1), :], (rows, 2 * LANES))
        rmat[pl.ds(first, rows), :] = pltpu.roll(line_k, 0, 1, stride=1, stride_axis=0).astype(BF16)
        for part in range(2):
            line_k = jnp.broadcast_to(base[1 + part, pl.ds(k, 1), :], (EXT, 2 * LANES))
            band = pltpu.roll(line_k, 0, 1, stride=1, stride_axis=0)
            for piece in range(2):
                if piece:
                    band = pltpu.roll(band, EXT, 1)
                bmat[k, piece * EXT:(piece + 1) * EXT, part * LANES:(part + 1) * LANES] = (
                    band[:, :LANES].astype(BF16)
                )

    @pl.when(q == 0)
    def _():
        for slot in range(slots):
            halo[slot, 0] = jnp.zeros((HALO, cols), F32)

    @pl.when(q == nq - 1)
    def _():
        for slot in range(slots):
            halo[slot, 1] = jnp.zeros((HALO, cols), F32)

    for copy in meta_copies:
        copy.wait()

    column = lax.broadcasted_iota(jnp.int32, (8, cols), 1)

    def owner(step, slot):
        def wide(place):
            value = metas[REACH + step, 3 * slot + place:3 * slot + place + 1, :]
            return jnp.concatenate([jnp.broadcast_to(value, (8, LANES))] * blocks, axis=1)
        return jnp.where(column >= wide(2), wide(0), wide(1))

    def group(part, g):
        return pl.ds(part * half + g * 8, 8)

    def part_rows(part):
        return pl.ds(part * half, half)

    for copy in hop1:
        copy.wait_recv()

    def second(d, slot, part):
        return remote(snd2.at[d, slot, part_rows(part)], r2.at[d, slot, part_rows(part)],
                      s2.at[d, slot, part], v2.at[d, slot, part], ahead[d])

    def third(d, slot, part):
        return remote(r2.at[d, slot, part_rows(part)], r3.at[d, slot, part_rows(part)],
                      s3.at[d, slot, part], v3.at[d, slot, part], ahead[d])

    def build(slot, part):
        for d, sign in enumerate(SIGN):
            wanted = owner(2 * sign, slot)
            source = at_visit(-sign)
            for g in range(groups):
                total = jnp.zeros((8, cols), F32)
                for t in range(slots):
                    total = jnp.where(wanted == slots * me + t, tiles[t, group(part, g), :], total)
                    total = jnp.where(wanted == slots * source + t, t1[d, t, group(part, g), :], total)
                snd2[d, slot, group(part, g), :] = total

    def start_second(slot, part):
        for d in range(2):
            second(d, slot, part).start()

    def relay(slot, part):
        for d, sign in enumerate(SIGN):
            wanted = owner(sign, slot)
            second(d, slot, part).wait_recv()
            for g in range(groups):
                total = r2[d, slot, group(part, g), :]
                for t in range(slots):
                    total = jnp.where(wanted == slots * me + t, tiles[t, group(part, g), :], total)
                r2[d, slot, group(part, g), :] = total
            third(d, slot, part).start()

    for part in range(2):
        build(0, part)
        start_second(0, part)
    for part in range(2):
        build(1, part)
    for part in range(2):
        relay(0, part)
    for part in range(2):
        start_second(1, part)

    def halo_copies(slot):
        down = remote(pre.at[slot, pl.ds(rows - HALO, HALO)], halo.at[slot, 0],
                      hs.at[slot, 0], hr.at[slot, 0], {"quad": at_quad(1)})
        up = remote(pre.at[slot, pl.ds(0, HALO)], halo.at[slot, 1],
                    hs.at[slot, 1], hr.at[slot, 1], {"quad": at_quad(nq - 1)})
        return down, up

    lane = lax.broadcasted_iota(jnp.int32, (HALO, LANES), 1)

    def spread(x, slot, first):
        shift = lax.rem(cols + taps // 2 - offs[slot], cols)
        x = pltpu.roll(x, shift, 1)
        head = x[:, :LANES]
        ext = jnp.concatenate(
            [jnp.where(lane >= taps // 2, head, 0.0), x[:, LANES:], jnp.where(lane < taps // 2, head, 0.0)],
            axis=1,
        )
        high, low = split(ext)
        width = cols + LANES
        tst[first:first + HALO, :width] = high
        tst[EXT + first:EXT + first + HALO, :width] = high
        tst[2 * EXT + first:2 * EXT + first + HALO, :width] = low

    own_row = lax.broadcasted_iota(jnp.int32, (32, LANES), 0)
    own_col = lax.broadcasted_iota(jnp.int32, (32, LANES), 1)

    def convolve(slot, events):
        for part in range(2):
            for d in range(2):
                third(d, slot, part).wait_recv()
        wanted = owner(0, slot)
        for g in range(rows // 8):
            sl = pl.ds(g * 8, 8)
            total = r3[0, slot, sl, :] + r3[1, slot, sl, :]
            for t in range(slots):
                total = jnp.where(wanted == slots * me + t, tiles[t, sl, :], total)
            pre[slot, sl, :] = total
        down, up = halo_copies(slot)

        @pl.when(q < nq - 1)
        def _():
            down.start()

        @pl.when(q > 0)
        def _():
            up.start()

        for g in range(rows // HALO):
            spread(pre[slot, g * HALO:(g + 1) * HALO, :], slot, HALO + g * HALO)

        @pl.when(q > 0)
        def _():
            down.wait_recv()

        @pl.when(q < nq - 1)
        def _():
            up.wait_recv()

        spread(halo[slot, 0], slot, 0)
        spread(halo[slot, 1], slot, HALO + rows)
        events[0]()

        chunk = count * HALO

        @pl.loop(0, (cols + 2 * LANES) // (2 * LANES))
        def _(n):
            sl = pl.ds(pl.multiple_of(n * 2 * LANES, 2 * LANES), 2 * LANES)
            weight = tst[:, sl]
            for piece in range(count * rows // chunk):
                rsl = pl.ds(piece * chunk, chunk)
                high, low = split(jnp.dot(rmat[rsl, :], weight, preferred_element_type=F32))
                yhi[rsl, sl] = high
                ylo[rsl, sl] = low

        events[1]()
        bounds = (0, 8, 16, 24, count)
        for segment in range(4):
            @pl.loop(bounds[segment], bounds[segment + 1])
            def _(k):
                rsl = pl.ds(pl.multiple_of(k * rows, 16), rows)
                left = jnp.concatenate(
                    [y[rsl, n * LANES:(n + 2) * LANES] for y in (yhi, ylo) for n in range(blocks)], axis=0
                )
                out = jnp.dot(left, bmat[k], preferred_element_type=F32)
                out = out[:, :LANES] + out[:, LANES:]
                out = out[:rows * blocks] + out[rows * blocks:]
                for n in range(blocks):
                    img[k, :, n * LANES:(n + 1) * LANES] = out[n * rows:(n + 1) * rows]
            events[2 + segment]()

        img[count] = sci[slot]
        gacc[...] = jnp.zeros_like(gacc)

        @pl.loop(0, rows // 8)
        def _(g):
            x = img[:, pl.ds(pl.multiple_of(g * 8, 8), 8), :].reshape(256, cols)
            high, low = split(x)
            both = jnp.concatenate([high, low], axis=0)
            gacc[...] += lax.dot_general(high, both, (((1,), (1,)), ((), ())), preferred_element_type=F32)

        srow = lax.broadcasted_iota(jnp.int32, (256, 256), 0)
        scol = lax.broadcasted_iota(jnp.int32, (256, 256), 1)
        same = lax.rem(srow, 8) == lax.rem(scol, 8)
        prow = lax.broadcasted_iota(jnp.int32, (256, LANES), 0)
        pcol = lax.broadcasted_iota(jnp.int32, (256, LANES), 1)
        gather = (lax.div(prow, 8) == pcol).astype(F32)

        def reduced(x):
            x = jnp.where(same, x, 0.0).reshape(32, 8, 256).sum(axis=1)
            return jnp.dot(x, gather, precision=HIGHEST, preferred_element_type=F32)

        main = reduced(gacc[:, :256])
        cross = reduced(gacc[:, 256:])
        square = jnp.concatenate([cross, jnp.zeros((96, LANES), F32)], axis=0)
        gbuf[slot, 0] = main + cross + square.T[:32]
        copies = [
            remote(gbuf.at[slot, 0], gbuf.at[slot, step], gs.at[slot, step - 1], gr.at[slot, step - 1],
                   {"quad": at_quad(step)})
            for step in range(1, nq)
        ]
        for copy in copies:
            copy.start()
        events[6]()
        for copy in copies:
            copy.wait_recv()
        total = gbuf[slot, lax.rem(q + nq, nq)]
        for source in range(1, nq):
            total = total + gbuf[slot, lax.rem(q + nq - source, nq)]
        system = total / pixels + jnp.where((own_row == own_col) & (own_col < count), 0.01, 0.0)
        for j in range(count):
            pivot_row = system[j:j + 1, :]
            pivot_col = jnp.broadcast_to(system[:, j:j + 1], (32, LANES))
            pivot = jnp.broadcast_to(system[j:j + 1, j:j + 1], (1, LANES))
            scaled = pivot_row * (1.0 / pivot)
            system = jnp.where(own_row == j, scaled, system - pivot_col * scaled)
        cs[...] = jnp.broadcast_to(system[:, count:count + 1], (32, LANES))

        @pl.loop(0, rows // 8)
        def _(g):
            sl = pl.ds(pl.multiple_of(g * 8, 8), 8)
            total = sci[slot, sl, :]
            for k in range(count):
                weight = jnp.broadcast_to(cs[k:k + 1, :], (8, LANES))
                total = total - jnp.concatenate([weight] * blocks, axis=1) * img[k, sl, :]
            diff[slot, sl, :] = total
            dt[slot, sl, :] = pltpu.roll(total, offs[slot], 1)

    def spread_copy(d, hop, slot, part):
        source = dt.at[slot, part_rows(part)] if hop == 0 else dbank.at[d, hop - 1, slot, part_rows(part)]
        return remote(source, dbank.at[d, hop, slot, part_rows(part)],
                      ds_.at[d, hop, slot, part], dr.at[d, hop, slot, part], ahead[d])

    def start_spread(slot):
        for part in range(2):
            for d in range(2):
                spread_copy(d, 0, slot, part).start()

    def forward(hop, slot, part):
        for d in range(2):
            spread_copy(d, hop, slot, part).wait_recv()
            if hop + 1 < REACH:
                spread_copy(d, hop + 1, slot, part).start()

    def add(step, slot, data, parts=(0, 1)):
        wanted = owner(step, slot)
        for part in parts:
            for g in range(groups):
                value = data[group(part, g), :]
                for t in range(slots):
                    coadd[t, group(part, g), :] += jnp.where(wanted == slots * me + t, value, 0.0)

    def nothing():
        pass

    relay_events = [nothing] * 7
    relay_events[1] = functools.partial(relay, 1, 0)
    relay_events[2] = functools.partial(relay, 1, 1)
    convolve(0, relay_events)
    start_spread(0)
    for t in range(slots):
        coadd[t] = jnp.zeros((rows, cols), F32)
    add(0, 0, dt.at[0])

    spread_events = [nothing] * 7
    spread_events[1] = functools.partial(forward, 0, 0, 0)
    spread_events[2] = functools.partial(forward, 0, 0, 1)
    spread_events[3] = functools.partial(forward, 1, 0, 0)
    spread_events[4] = functools.partial(forward, 1, 0, 1)
    convolve(1, spread_events)
    start_spread(1)
    add(0, 1, dt.at[1])
    for d, sign in enumerate(SIGN):
        add(-sign, 0, dbank.at[d, 0, 0])
    forward(0, 1, 0)
    forward(0, 1, 1)
    for d, sign in enumerate(SIGN):
        add(-2 * sign, 0, dbank.at[d, 1, 0])
    forward(1, 1, 0)
    forward(1, 1, 1)
    forward(2, 0, 0)
    forward(2, 0, 1)
    for d, sign in enumerate(SIGN):
        add(-3 * sign, 0, dbank.at[d, 2, 0])
        add(-sign, 1, dbank.at[d, 0, 1])
        add(-2 * sign, 1, dbank.at[d, 1, 1])
    for part in range(2):
        forward(2, 1, part)
        for d, sign in enumerate(SIGN):
            add(-3 * sign, 1, dbank.at[d, 2, 1], (part,))

    for copy in hop1:
        copy.wait_send()
    for slot in range(slots):
        down, up = halo_copies(slot)

        @pl.when(q < nq - 1)
        def _():
            down.wait_send()

        @pl.when(q > 0)
        def _():
            up.wait_send()

        for step in range(1, nq):
            remote(gbuf.at[slot, 0], gbuf.at[slot, step], gs.at[slot, step - 1], gr.at[slot, step - 1],
                   {"quad": at_quad(step)}).wait_send()
        for part in range(2):
            for d in range(2):
                second(d, slot, part).wait_send()
                third(d, slot, part).wait_send()
                for hop in range(REACH):
                    spread_copy(d, hop, slot, part).wait_send()


def on_device(science, reference_tiles, visit_tiles, offsets, basis_rows, basis_cols):
    slots, rows, cols = science.shape
    count = basis_rows.shape[0]
    nq = lax.axis_size("quad")
    pixels = nq * rows * cols
    pad = ((0, 32 - count), (0, LANES - basis_rows.shape[1]))
    brow = jnp.pad(basis_rows, pad)
    bcol = jnp.pad(basis_cols[:, ::-1], pad)
    vmem = pl.BlockSpec(memory_space=pltpu.VMEM)
    smem = pl.BlockSpec(memory_space=pltpu.SMEM)
    dma = pltpu.SemaphoreType.DMA
    ext_cols = cols + 2 * LANES
    return pl.pallas_call(
        functools.partial(kernel, float(pixels)),
        out_shape=[jax.ShapeDtypeStruct((slots, rows, cols), F32)] * 2,
        in_specs=[vmem, vmem, smem, smem, vmem, vmem],
        out_specs=[vmem, vmem],
        scratch_shapes=[
            pltpu.VMEM((2 * REACH + 1, 8, LANES), jnp.int32),
            pltpu.VMEM((2, slots, rows, cols), F32),
            pltpu.VMEM((2, slots, rows, cols), F32),
            pltpu.VMEM((2, slots, rows, cols), F32),
            pltpu.VMEM((2, slots, rows, cols), F32),
            pltpu.VMEM((slots, rows, cols), F32),
            pltpu.VMEM((slots, 2, HALO, cols), F32),
            pltpu.VMEM((256, ext_cols), BF16),
            pltpu.VMEM((count * rows, 256), BF16),
            pltpu.VMEM((3, 32, 256), F32),
            pltpu.VMEM((count, 256, 256), BF16),
            pltpu.VMEM((count * rows, ext_cols), BF16),
            pltpu.VMEM((count * rows, ext_cols), BF16),
            pltpu.VMEM((count + 1, rows, cols), F32),
            pltpu.VMEM((256, 512), F32),
            pltpu.VMEM((slots, nq, 32, LANES), F32),
            pltpu.VMEM((32, LANES), F32),
            pltpu.VMEM((slots, rows, cols), F32),
            pltpu.VMEM((2, REACH, slots, rows, cols), F32),
            dma((2 * REACH + 1,)), dma((2 * REACH + 1,)),
            dma((2, slots)), dma((2, slots)),
            dma((2, slots, 2)), dma((2, slots, 2)),
            dma((2, slots, 2)), dma((2, slots, 2)),
            dma((slots, 2)), dma((slots, 2)),
            dma((slots, nq - 1)), dma((slots, nq - 1)),
            dma((2, REACH, slots, 2)), dma((2, REACH, slots, 2)),
        ],
        compiler_params=pltpu.CompilerParams(
            collective_id=0, has_side_effects=True, vmem_limit_bytes=56 * 1024 * 1024
        ),
        cost_estimate=pl.CostEstimate(flops=8_000_000_000, bytes_accessed=2_000_000, transcendentals=0),
    )(science, reference_tiles, visit_tiles, offsets, brow, bcol)


def solution(mesh):
    tiles = P("visit", "quad", None)
    return jax.shard_map(
        on_device,
        mesh=mesh,
        in_specs=(tiles, tiles, P("visit", None), P("visit"), P(), P()),
        out_specs=(tiles, tiles),
        check_vma=False,
    )
```

```python
import functools

import jax
import jax.numpy as jnp
from jax import lax
from jax.experimental import pallas as pl
from jax.experimental.pallas import tpu as pltpu
from jax.sharding import PartitionSpec as P

MESH = pl.DeviceIdType.MESH
REACH = 3
LANES = 128
HALO = 16
CHUNKS = 3
EXT = 80
HIGHEST = lax.Precision.HIGHEST
F32 = jnp.float32
BF16 = jnp.bfloat16
SIGN = (1, -1)


def split(x):
    high = x.astype(BF16)
    return high, (x - high.astype(F32)).astype(BF16)


def kernel(
    pixels,
    sci, tiles, pairs, offs, brow, bcol,
    diff, coadd,
    metas, bank, pre, halo, tst, rmat, base, bmat, yhi, ylo, img,
    gacc, gbuf, cs, dt, dbank,
    ms, mr, ts, tr, hs, hr, gs, gr, ds_, dr,
):
    slots, rows, cols = sci.shape
    taps = 31
    count = 31
    chunk_rows = rows // CHUNKS
    nv, nq = lax.axis_size("visit"), lax.axis_size("quad")
    me, q = lax.axis_index("visit"), lax.axis_index("quad")
    blocks = cols // LANES
    groups = chunk_rows // 8

    def at_visit(step):
        return lax.rem(me + step + nv, nv)

    def at_quad(step):
        return lax.rem(q + step, nq)

    def remote(src, dst, send, recv, device):
        return pltpu.make_async_remote_copy(
            src_ref=src, dst_ref=dst, send_sem=send, recv_sem=recv,
            device_id=device, device_id_type=MESH,
        )

    steps = [step * sign for step in range(1, REACH + 1) for sign in SIGN]
    barrier = pltpu.get_barrier_semaphore()
    for step in steps:
        pl.semaphore_signal(barrier, inc=1, device_id={"visit": at_visit(step)}, device_id_type=MESH)
    for step in range(1, nq):
        pl.semaphore_signal(barrier, inc=1, device_id={"quad": at_quad(step)}, device_id_type=MESH)

    line = lax.broadcasted_iota(jnp.int32, (8, LANES), 0)
    own = jnp.zeros((8, LANES), jnp.int32)
    for slot in range(slots):
        for place, value in enumerate((pairs[slot, 0], pairs[slot, 1], offs[slot])):
            own = jnp.where(line == 3 * slot + place, value, own)
    metas[REACH] = own
    pl.semaphore_wait(barrier, len(steps) + nq - 1)

    meta_copies = [
        remote(metas.at[REACH], metas.at[REACH - step], ms.at[REACH - step], mr.at[REACH - step],
               {"visit": at_visit(step)})
        for step in steps
    ]
    for copy in meta_copies:
        copy.start()
    ahead = [{"visit": at_visit(sign)} for sign in SIGN]
    tst[...] = jnp.zeros_like(tst)
    bmat[...] = jnp.zeros_like(bmat)
    blank = jnp.zeros((32, LANES), F32)
    row_high = brow[...].astype(BF16).astype(F32)
    row_low = brow[...] - row_high
    wide_high = jnp.concatenate([row_high, blank], axis=1)
    wide_low = jnp.concatenate([row_low, blank], axis=1)
    base[0] = (
        pltpu.roll(wide_high, 1, 1) + pltpu.roll(wide_low, EXT + 1, 1) + pltpu.roll(wide_high, 2 * EXT + 1, 1)
    )
    col_high = bcol[...].astype(BF16).astype(F32)
    back = 2 * LANES - (taps - 1)
    base[1] = pltpu.roll(jnp.concatenate([col_high, blank], axis=1), back, 1)
    base[2] = pltpu.roll(jnp.concatenate([bcol[...] - col_high, blank], axis=1), back, 1)

    @pl.loop(0, count)
    def _(k):
        first = pl.multiple_of(k * rows, 16)
        line_k = jnp.broadcast_to(base[0, pl.ds(k, 1), :], (rows, 2 * LANES))
        rmat[pl.ds(first, rows), :] = pltpu.roll(line_k, 0, 1, stride=1, stride_axis=0).astype(BF16)

    def bands(first, last):
        @pl.loop(first, last)
        def _(k):
            for part in range(2):
                line_k = jnp.broadcast_to(base[1 + part, pl.ds(k, 1), :], (EXT, 2 * LANES))
                band = pltpu.roll(line_k, 0, 1, stride=1, stride_axis=0)
                for piece in range(2):
                    if piece:
                        band = pltpu.roll(band, EXT, 1)
                    bmat[k, piece * EXT:(piece + 1) * EXT, part * LANES:(part + 1) * LANES] = (
                        band[:, :LANES].astype(BF16)
                    )

    @pl.when(q == 0)
    def _():
        for slot in range(slots):
            halo[slot, 0] = jnp.zeros((HALO, cols), F32)

    @pl.when(q == nq - 1)
    def _():
        for slot in range(slots):
            halo[slot, 1] = jnp.zeros((HALO, cols), F32)

    for copy in meta_copies:
        copy.wait()

    column = lax.broadcasted_iota(jnp.int32, (8, cols), 1)

    def owner(step, slot):
        def wide(place):
            value = metas[REACH + step, 3 * slot + place:3 * slot + place + 1, :]
            return jnp.concatenate([jnp.broadcast_to(value, (8, LANES))] * blocks, axis=1)
        return jnp.where(column >= wide(2), wide(0), wide(1))

    def group(part, g):
        return pl.ds(part * chunk_rows + g * 8, 8)

    def part_rows(part):
        return pl.ds(part * chunk_rows, chunk_rows)

    def hop_copy(d, hop, slot, part):
        return remote(bank.at[hop - 1, d, slot, part_rows(part)], bank.at[hop, d, slot, part_rows(part)],
                      ts.at[hop - 1, d, slot, part], tr.at[hop - 1, d, slot, part], ahead[d])

    def relay(hop, slot, part):
        for d, sign in enumerate(SIGN):
            wanted = owner((REACH - hop) * sign, slot)
            if hop:
                hop_copy(d, hop, slot, part).wait_recv()
            for g in range(groups):
                sl = group(part, g)
                total = bank[hop, d, slot, sl, :] if hop else jnp.zeros((8, cols), F32)
                for t in range(slots):
                    total = jnp.where(wanted == slots * me + t, tiles[t, sl, :], total)
                bank[hop, d, slot, sl, :] = total
            hop_copy(d, hop + 1, slot, part).start()

    def halo_copies(slot):
        down = remote(pre.at[slot, pl.ds(rows - HALO, HALO)], halo.at[slot, 0],
                      hs.at[slot, 0], hr.at[slot, 0], {"quad": at_quad(1)})
        up = remote(pre.at[slot, pl.ds(0, HALO)], halo.at[slot, 1],
                    hs.at[slot, 1], hr.at[slot, 1], {"quad": at_quad(nq - 1)})
        return down, up

    lane = lax.broadcasted_iota(jnp.int32, (HALO, LANES), 1)

    def spread(x, slot, first):
        shift = lax.rem(cols + taps // 2 - offs[slot], cols)
        x = pltpu.roll(x, shift, 1)
        head = x[:, :LANES]
        ext = jnp.concatenate(
            [jnp.where(lane >= taps // 2, head, 0.0), x[:, LANES:], jnp.where(lane < taps // 2, head, 0.0)],
            axis=1,
        )
        high, low = split(ext)
        width = cols + LANES
        tst[first:first + HALO, :width] = high
        tst[EXT + first:EXT + first + HALO, :width] = high
        tst[2 * EXT + first:2 * EXT + first + HALO, :width] = low

    own_row = lax.broadcasted_iota(jnp.int32, (32, LANES), 0)
    own_col = lax.broadcasted_iota(jnp.int32, (32, LANES), 1)

    def gram_copies(slot):
        return [
            remote(gbuf.at[slot, 0], gbuf.at[slot, step], gs.at[slot, step - 1], gr.at[slot, step - 1],
                   {"quad": at_quad(step)})
            for step in range(1, nq)
        ]

    def assemble(slot):
        for part in range(CHUNKS):
            for d in range(2):
                hop_copy(d, REACH, slot, part).wait_recv()
        wanted = owner(0, slot)
        for g in range(rows // 8):
            sl = pl.ds(g * 8, 8)
            total = bank[REACH, 0, slot, sl, :] + bank[REACH, 1, slot, sl, :]
            for t in range(slots):
                total = jnp.where(wanted == slots * me + t, tiles[t, sl, :], total)
            pre[slot, sl, :] = total
        down, up = halo_copies(slot)

        @pl.when(q < nq - 1)
        def _():
            down.start()

        @pl.when(q > 0)
        def _():
            up.start()

        for g in range(rows // HALO):
            spread(pre[slot, g * HALO:(g + 1) * HALO, :], slot, HALO + g * HALO)

    def edges(slot):
        down, up = halo_copies(slot)

        @pl.when(q > 0)
        def _():
            down.wait_recv()

        @pl.when(q < nq - 1)
        def _():
            up.wait_recv()

        spread(halo[slot, 0], slot, 0)
        spread(halo[slot, 1], slot, HALO + rows)

    def row_step():
        chunk = count * HALO

        @pl.loop(0, (cols + 2 * LANES) // (2 * LANES), unroll=True)
        def _(n):
            sl = pl.ds(pl.multiple_of(n * 2 * LANES, 2 * LANES), 2 * LANES)
            weight = tst[:, sl]
            for piece in range(count * rows // chunk):
                rsl = pl.ds(piece * chunk, chunk)
                high, low = split(jnp.dot(rmat[rsl, :], weight, preferred_element_type=F32))
                yhi[rsl, sl] = high
                ylo[rsl, sl] = low

    bounds = (0, 8, 16, 24, count)

    def column_step(segment):
        @pl.loop(bounds[segment], bounds[segment + 1], unroll=True)
        def _(k):
            rsl = pl.ds(pl.multiple_of(k * rows, 16), rows)
            left = jnp.concatenate(
                [y[rsl, n * LANES:(n + 2) * LANES] for y in (yhi, ylo) for n in range(blocks)], axis=0
            )
            out = jnp.dot(left, bmat[k], preferred_element_type=F32)
            out = out[:, :LANES] + out[:, LANES:]
            out = out[:rows * blocks] + out[rows * blocks:]
            for n in range(blocks):
                img[k, :, n * LANES:(n + 1) * LANES] = out[n * rows:(n + 1) * rows]

    def products(slot):
        img[count] = sci[slot]
        gacc[...] = jnp.zeros_like(gacc)

        @pl.loop(0, rows // 8, unroll=True)
        def _(g):
            x = img[:, pl.ds(pl.multiple_of(g * 8, 8), 8), :].reshape(256, cols)
            high, low = split(x)
            gacc[:, :256] += lax.dot_general(high, high, (((1,), (1,)), ((), ())), preferred_element_type=F32)
            gacc[:, 256:] += lax.dot_general(high, low, (((1,), (1,)), ((), ())), preferred_element_type=F32)

        srow = lax.broadcasted_iota(jnp.int32, (256, 256), 0)
        scol = lax.broadcasted_iota(jnp.int32, (256, 256), 1)
        same = lax.rem(srow, 8) == lax.rem(scol, 8)
        prow = lax.broadcasted_iota(jnp.int32, (256, LANES), 0)
        pcol = lax.broadcasted_iota(jnp.int32, (256, LANES), 1)
        gather = (lax.div(prow, 8) == pcol).astype(F32)

        def reduced(x):
            x = jnp.where(same, x, 0.0).reshape(32, 8, 256).sum(axis=1)
            return jnp.dot(x, gather, precision=HIGHEST, preferred_element_type=F32)

        main = reduced(gacc[:, :256])
        cross = reduced(gacc[:, 256:])
        square = jnp.concatenate([cross, jnp.zeros((96, LANES), F32)], axis=0)
        gbuf[slot, 0] = main + cross + square.T[:32]
        for copy in gram_copies(slot):
            copy.start()

    def solve(slot, middle):
        for copy in gram_copies(slot):
            copy.wait_recv()
        total = gbuf[slot, lax.rem(q + nq, nq)]
        for source in range(1, nq):
            total = total + gbuf[slot, lax.rem(q + nq - source, nq)]
        system = total / pixels + jnp.where((own_row == own_col) & (own_col < count), 0.01, 0.0)
        for j in range(count):
            if j == count // 2:
                middle()
            pivot_row = system[j:j + 1, :]
            pivot_col = jnp.broadcast_to(system[:, j:j + 1], (32, LANES))
            pivot = jnp.broadcast_to(system[j:j + 1, j:j + 1], (1, LANES))
            scaled = pivot_row * (1.0 / pivot)
            system = jnp.where(own_row == j, scaled, system - pivot_col * scaled)
        cs[...] = jnp.broadcast_to(system[:, count:count + 1], (32, LANES))

    def subtract(slot):
        @pl.loop(0, rows // 8, unroll=True)
        def _(g):
            sl = pl.ds(pl.multiple_of(g * 8, 8), 8)
            total = sci[slot, sl, :]
            for k in range(count):
                weight = jnp.broadcast_to(cs[k:k + 1, :], (8, LANES))
                total = total - jnp.concatenate([weight] * blocks, axis=1) * img[k, sl, :]
            diff[slot, sl, :] = total
            dt[slot, sl, :] = pltpu.roll(total, offs[slot], 1)

    def spread_copy(d, hop, slot, part):
        source = dt.at[slot, part_rows(part)] if hop == 0 else dbank.at[d, hop - 1, slot, part_rows(part)]
        return remote(source, dbank.at[d, hop, slot, part_rows(part)],
                      ds_.at[d, hop, slot, part], dr.at[d, hop, slot, part], ahead[d])

    def start_spread(slot):
        for part in range(CHUNKS):
            for d in range(2):
                spread_copy(d, 0, slot, part).start()

    def forward(hop, slot, part):
        for d in range(2):
            spread_copy(d, hop, slot, part).wait_recv()
            if hop + 1 < REACH:
                spread_copy(d, hop + 1, slot, part).start()

    def add(step, slot, data, parts=range(CHUNKS)):
        wanted = owner(step, slot)
        for part in parts:
            for g in range(groups):
                value = data[group(part, g), :]
                for t in range(slots):
                    coadd[t, group(part, g), :] += jnp.where(wanted == slots * me + t, value, 0.0)

    def nothing():
        pass

    for part in range(CHUNKS):
        relay(0, 0, part)
    bands(0, 16)
    for part in range(CHUNKS):
        relay(1, 0, part)
    bands(16, 24)
    for part in range(CHUNKS):
        relay(2, 0, part)
    for part in range(CHUNKS):
        relay(0, 1, part)
    bands(24, count)
    for t in range(slots):
        coadd[t] = jnp.zeros((rows, cols), F32)

    assemble(0)
    relay(1, 1, 0)
    relay(1, 1, 1)
    edges(0)
    row_step()
    relay(1, 1, 2)
    column_step(0)
    relay(2, 1, 0)
    column_step(1)
    relay(2, 1, 1)
    column_step(2)
    relay(2, 1, 2)
    column_step(3)
    products(0)
    assemble(1)
    solve(0, nothing)
    subtract(0)
    start_spread(0)

    edges(1)
    row_step()
    column_step(0)
    column_step(1)
    column_step(2)
    forward(0, 0, 0)
    column_step(3)
    forward(0, 0, 1)
    products(1)
    add(0, 0, dt.at[0])
    forward(0, 0, 2)
    forward(1, 0, 0)
    forward(1, 0, 1)
    solve(1, functools.partial(forward, 1, 0, 2))
    subtract(1)
    start_spread(1)

    add(0, 1, dt.at[1])
    for d, sign in enumerate(SIGN):
        add(-sign, 0, dbank.at[d, 0, 0])
    for part in range(CHUNKS):
        forward(0, 1, part)
    for d, sign in enumerate(SIGN):
        add(-2 * sign, 0, dbank.at[d, 1, 0])
    for part in range(CHUNKS):
        forward(1, 1, part)
    for part in range(CHUNKS):
        forward(2, 0, part)
    for d, sign in enumerate(SIGN):
        add(-3 * sign, 0, dbank.at[d, 2, 0])
        add(-sign, 1, dbank.at[d, 0, 1])
        add(-2 * sign, 1, dbank.at[d, 1, 1])
    for part in range(CHUNKS):
        forward(2, 1, part)
        for d, sign in enumerate(SIGN):
            add(-3 * sign, 1, dbank.at[d, 2, 1], (part,))

    for slot in range(slots):
        down, up = halo_copies(slot)

        @pl.when(q < nq - 1)
        def _():
            down.wait_send()

        @pl.when(q > 0)
        def _():
            up.wait_send()

        for copy in gram_copies(slot):
            copy.wait_send()
        for part in range(CHUNKS):
            for d in range(2):
                for hop in range(REACH):
                    hop_copy(d, hop + 1, slot, part).wait_send()
                    spread_copy(d, hop, slot, part).wait_send()


def on_device(science, reference_tiles, visit_tiles, offsets, basis_rows, basis_cols):
    slots, rows, cols = science.shape
    count = basis_rows.shape[0]
    nq = lax.axis_size("quad")
    pixels = nq * rows * cols
    pad = ((0, 32 - count), (0, LANES - basis_rows.shape[1]))
    brow = jnp.pad(basis_rows, pad)
    bcol = jnp.pad(basis_cols[:, ::-1], pad)
    vmem = pl.BlockSpec(memory_space=pltpu.VMEM)
    smem = pl.BlockSpec(memory_space=pltpu.SMEM)
    dma = pltpu.SemaphoreType.DMA
    ext_cols = cols + 2 * LANES
    return pl.pallas_call(
        functools.partial(kernel, float(pixels)),
        out_shape=[jax.ShapeDtypeStruct((slots, rows, cols), F32)] * 2,
        in_specs=[vmem, vmem, smem, smem, vmem, vmem],
        out_specs=[vmem, vmem],
        scratch_shapes=[
            pltpu.VMEM((2 * REACH + 1, 8, LANES), jnp.int32),
            pltpu.VMEM((REACH + 1, 2, slots, rows, cols), F32),
            pltpu.VMEM((slots, rows, cols), F32),
            pltpu.VMEM((slots, 2, HALO, cols), F32),
            pltpu.VMEM((256, ext_cols), BF16),
            pltpu.VMEM((count * rows, 256), BF16),
            pltpu.VMEM((3, 32, 256), F32),
            pltpu.VMEM((count, 256, 256), BF16),
            pltpu.VMEM((count * rows, ext_cols), BF16),
            pltpu.VMEM((count * rows, ext_cols), BF16),
            pltpu.VMEM((count + 1, rows, cols), F32),
            pltpu.VMEM((256, 512), F32),
            pltpu.VMEM((slots, nq, 32, LANES), F32),
            pltpu.VMEM((32, LANES), F32),
            pltpu.VMEM((slots, rows, cols), F32),
            pltpu.VMEM((2, REACH, slots, rows, cols), F32),
            dma((2 * REACH + 1,)), dma((2 * REACH + 1,)),
            dma((REACH, 2, slots, CHUNKS)), dma((REACH, 2, slots, CHUNKS)),
            dma((slots, 2)), dma((slots, 2)),
            dma((slots, nq - 1)), dma((slots, nq - 1)),
            dma((2, REACH, slots, CHUNKS)), dma((2, REACH, slots, CHUNKS)),
        ],
        compiler_params=pltpu.CompilerParams(
            collective_id=0, has_side_effects=True, vmem_limit_bytes=56 * 1024 * 1024
        ),
        cost_estimate=pl.CostEstimate(flops=8_000_000_000, bytes_accessed=2_000_000, transcendentals=0),
    )(science, reference_tiles, visit_tiles, offsets, brow, bcol)


def solution(mesh):
    tiles = P("visit", "quad", None)
    return jax.shard_map(
        on_device,
        mesh=mesh,
        in_specs=(tiles, tiles, P("visit", None), P("visit"), P(), P()),
        out_specs=(tiles, tiles),
        check_vma=False,
    )
```

```python
import functools

import jax
import jax.numpy as jnp
from jax import lax
from jax.experimental import pallas as pl
from jax.experimental.pallas import tpu as pltpu
from jax.sharding import PartitionSpec as P

MESH = pl.DeviceIdType.MESH
REACH = 3
LANES = 128
HALO = 16
CHUNKS = 3
EXT = 80
HIGHEST = lax.Precision.HIGHEST
F32 = jnp.float32
BF16 = jnp.bfloat16
SIGN = (1, -1)


def split(x):
    high = x.astype(BF16)
    return high, (x - high.astype(F32)).astype(BF16)


def kernel(
    pixels,
    sci, tiles, pairs, offs, brow, bcol,
    diff, coadd,
    metas, bank, pre, halo, tst, rmat, base, bmat, yhi, ylo, img,
    gacc, gbuf, cs, dt, dbank,
    ms, mr, ts, tr, hs, hr, gs, gr, ds_, dr,
):
    slots, rows, cols = sci.shape
    taps = 31
    count = 31
    chunk_rows = rows // CHUNKS
    nv, nq = lax.axis_size("visit"), lax.axis_size("quad")
    me, q = lax.axis_index("visit"), lax.axis_index("quad")
    blocks = cols // LANES
    groups = chunk_rows // 8

    def at_visit(step):
        return lax.rem(me + step + nv, nv)

    def at_quad(step):
        return lax.rem(q + step, nq)

    def remote(src, dst, send, recv, device):
        return pltpu.make_async_remote_copy(
            src_ref=src, dst_ref=dst, send_sem=send, recv_sem=recv,
            device_id=device, device_id_type=MESH,
        )

    steps = [step * sign for step in range(1, REACH + 1) for sign in SIGN]
    barrier = pltpu.get_barrier_semaphore()
    for step in steps:
        pl.semaphore_signal(barrier, inc=1, device_id={"visit": at_visit(step)}, device_id_type=MESH)
    for step in range(1, nq):
        pl.semaphore_signal(barrier, inc=1, device_id={"quad": at_quad(step)}, device_id_type=MESH)

    line = lax.broadcasted_iota(jnp.int32, (8, LANES), 0)
    own = jnp.zeros((8, LANES), jnp.int32)
    for slot in range(slots):
        for place, value in enumerate((pairs[slot, 0], pairs[slot, 1], offs[slot])):
            own = jnp.where(line == 3 * slot + place, value, own)
    metas[REACH] = own
    pl.semaphore_wait(barrier, len(steps) + nq - 1)

    meta_copies = [
        remote(metas.at[REACH], metas.at[REACH - step], ms.at[REACH - step], mr.at[REACH - step],
               {"visit": at_visit(step)})
        for step in steps
    ]
    for copy in meta_copies:
        copy.start()
    ahead = [{"visit": at_visit(sign)} for sign in SIGN]
    tst[...] = jnp.zeros_like(tst)
    bmat[...] = jnp.zeros_like(bmat)
    blank = jnp.zeros((32, LANES), F32)
    row_high = brow[...].astype(BF16).astype(F32)
    row_low = brow[...] - row_high
    wide_high = jnp.concatenate([row_high, blank], axis=1)
    wide_low = jnp.concatenate([row_low, blank], axis=1)
    base[0] = (
        pltpu.roll(wide_high, 1, 1) + pltpu.roll(wide_low, EXT + 1, 1) + pltpu.roll(wide_high, 2 * EXT + 1, 1)
    )
    col_high = bcol[...].astype(BF16).astype(F32)
    back = 2 * LANES - (taps - 1)
    base[1] = pltpu.roll(jnp.concatenate([col_high, blank], axis=1), back, 1)
    base[2] = pltpu.roll(jnp.concatenate([bcol[...] - col_high, blank], axis=1), back, 1)

    @pl.loop(0, count)
    def _(k):
        first = pl.multiple_of(k * rows, 16)
        line_k = jnp.broadcast_to(base[0, pl.ds(k, 1), :], (rows, 2 * LANES))
        rmat[pl.ds(first, rows), :] = pltpu.roll(line_k, 0, 1, stride=1, stride_axis=0).astype(BF16)

    def bands(first, last):
        @pl.loop(first, last)
        def _(k):
            for part in range(2):
                line_k = jnp.broadcast_to(base[1 + part, pl.ds(k, 1), :], (EXT, 2 * LANES))
                band = pltpu.roll(line_k, 0, 1, stride=1, stride_axis=0)
                for piece in range(2):
                    if piece:
                        band = pltpu.roll(band, EXT, 1)
                    bmat[k, piece * EXT:(piece + 1) * EXT, part * LANES:(part + 1) * LANES] = (
                        band[:, :LANES].astype(BF16)
                    )

    @pl.when(q == 0)
    def _():
        for slot in range(slots):
            halo[slot, 0] = jnp.zeros((HALO, cols), F32)

    @pl.when(q == nq - 1)
    def _():
        for slot in range(slots):
            halo[slot, 1] = jnp.zeros((HALO, cols), F32)

    for copy in meta_copies:
        copy.wait()

    column = lax.broadcasted_iota(jnp.int32, (8, cols), 1)

    def owner(step, slot):
        def wide(place):
            value = metas[REACH + step, 3 * slot + place:3 * slot + place + 1, :]
            return jnp.concatenate([jnp.broadcast_to(value, (8, LANES))] * blocks, axis=1)
        return jnp.where(column >= wide(2), wide(0), wide(1))

    def group(part, g):
        return pl.ds(part * chunk_rows + g * 8, 8)

    def part_rows(part):
        return pl.ds(part * chunk_rows, chunk_rows)

    def hop_copy(d, hop, slot, part):
        return remote(bank.at[hop - 1, d, slot, part_rows(part)], bank.at[hop, d, slot, part_rows(part)],
                      ts.at[hop - 1, d, slot, part], tr.at[hop - 1, d, slot, part], ahead[d])

    def relay(hop, slot, part):
        for d, sign in enumerate(SIGN):
            wanted = owner((REACH - hop) * sign, slot)
            if hop:
                hop_copy(d, hop, slot, part).wait_recv()
            for g in range(groups):
                sl = group(part, g)
                total = bank[hop, d, slot, sl, :] if hop else jnp.zeros((8, cols), F32)
                for t in range(slots):
                    total = jnp.where(wanted == slots * me + t, tiles[t, sl, :], total)
                bank[hop, d, slot, sl, :] = total
            hop_copy(d, hop + 1, slot, part).start()

    def halo_copies(slot):
        down = remote(pre.at[slot, pl.ds(rows - HALO, HALO)], halo.at[slot, 0],
                      hs.at[slot, 0], hr.at[slot, 0], {"quad": at_quad(1)})
        up = remote(pre.at[slot, pl.ds(0, HALO)], halo.at[slot, 1],
                    hs.at[slot, 1], hr.at[slot, 1], {"quad": at_quad(nq - 1)})
        return down, up

    lane = lax.broadcasted_iota(jnp.int32, (HALO, LANES), 1)

    def spread(x, slot, first):
        shift = lax.rem(cols + taps // 2 - offs[slot], cols)
        x = pltpu.roll(x, shift, 1)
        head = x[:, :LANES]
        ext = jnp.concatenate(
            [jnp.where(lane >= taps // 2, head, 0.0), x[:, LANES:], jnp.where(lane < taps // 2, head, 0.0)],
            axis=1,
        )
        high, low = split(ext)
        width = cols + LANES
        tst[first:first + HALO, :width] = high
        tst[EXT + first:EXT + first + HALO, :width] = high
        tst[2 * EXT + first:2 * EXT + first + HALO, :width] = low

    own_row = lax.broadcasted_iota(jnp.int32, (32, LANES), 0)
    own_col = lax.broadcasted_iota(jnp.int32, (32, LANES), 1)

    def gram_copies(slot):
        return [
            remote(gbuf.at[slot, 0], gbuf.at[slot, step], gs.at[slot, step - 1], gr.at[slot, step - 1],
                   {"quad": at_quad(step)})
            for step in range(1, nq)
        ]

    def assemble(slot):
        for part in range(CHUNKS):
            for d in range(2):
                hop_copy(d, REACH, slot, part).wait_recv()
        wanted = owner(0, slot)
        for g in range(rows // 8):
            sl = pl.ds(g * 8, 8)
            total = bank[REACH, 0, slot, sl, :] + bank[REACH, 1, slot, sl, :]
            for t in range(slots):
                total = jnp.where(wanted == slots * me + t, tiles[t, sl, :], total)
            pre[slot, sl, :] = total
        down, up = halo_copies(slot)

        @pl.when(q < nq - 1)
        def _():
            down.start()

        @pl.when(q > 0)
        def _():
            up.start()

        for g in range(rows // HALO):
            spread(pre[slot, g * HALO:(g + 1) * HALO, :], slot, HALO + g * HALO)

    def edges(slot):
        down, up = halo_copies(slot)

        @pl.when(q > 0)
        def _():
            down.wait_recv()

        @pl.when(q < nq - 1)
        def _():
            up.wait_recv()

        spread(halo[slot, 0], slot, 0)
        spread(halo[slot, 1], slot, HALO + rows)

    def row_step():
        chunk = count * HALO

        @pl.loop(0, (cols + 2 * LANES) // (2 * LANES), unroll=True)
        def _(n):
            sl = pl.ds(pl.multiple_of(n * 2 * LANES, 2 * LANES), 2 * LANES)
            weight = tst[:, sl]
            for piece in range(count * rows // chunk):
                rsl = pl.ds(piece * chunk, chunk)
                high, low = split(jnp.dot(rmat[rsl, :], weight, preferred_element_type=F32))
                yhi[rsl, sl] = high
                ylo[rsl, sl] = low

    bounds = (0, 8, 16, 24, count)

    def column_step(segment):
        @pl.loop(bounds[segment], bounds[segment + 1], unroll=True)
        def _(k):
            rsl = pl.ds(pl.multiple_of(k * rows, 16), rows)
            left = jnp.concatenate(
                [y[rsl, n * LANES:(n + 2) * LANES] for y in (yhi, ylo) for n in range(blocks)], axis=0
            )
            out = jnp.dot(left, bmat[k], preferred_element_type=F32)
            out = out[:, :LANES] + out[:, LANES:]
            out = out[:rows * blocks] + out[rows * blocks:]
            for n in range(blocks):
                img[k, :, n * LANES:(n + 1) * LANES] = out[n * rows:(n + 1) * rows]

    def products(slot):
        img[count] = sci[slot]
        gacc[...] = jnp.zeros_like(gacc)

        @pl.loop(0, rows // 8, unroll=True)
        def _(g):
            x = img[:, pl.ds(pl.multiple_of(g * 8, 8), 8), :].reshape(256, cols)
            high, low = split(x)
            gacc[:, :256] += lax.dot_general(high, high, (((1,), (1,)), ((), ())), preferred_element_type=F32)
            gacc[:, 256:] += lax.dot_general(high, low, (((1,), (1,)), ((), ())), preferred_element_type=F32)

        srow = lax.broadcasted_iota(jnp.int32, (256, 256), 0)
        scol = lax.broadcasted_iota(jnp.int32, (256, 256), 1)
        same = lax.rem(srow, 8) == lax.rem(scol, 8)
        prow = lax.broadcasted_iota(jnp.int32, (256, LANES), 0)
        pcol = lax.broadcasted_iota(jnp.int32, (256, LANES), 1)
        gather = (lax.div(prow, 8) == pcol).astype(F32)

        def reduced(x):
            x = jnp.where(same, x, 0.0).reshape(32, 8, 256).sum(axis=1)
            return jnp.dot(x, gather, precision=HIGHEST, preferred_element_type=F32)

        main = reduced(gacc[:, :256])
        cross = reduced(gacc[:, 256:])
        square = jnp.concatenate([cross, jnp.zeros((96, LANES), F32)], axis=0)
        gbuf[slot, 0] = main + cross + square.T[:32]
        for copy in gram_copies(slot):
            copy.start()

    def solve(slot, middle):
        for copy in gram_copies(slot):
            copy.wait_recv()
        total = gbuf[slot, lax.rem(q + nq, nq)]
        for source in range(1, nq):
            total = total + gbuf[slot, lax.rem(q + nq - source, nq)]
        system = total / pixels + jnp.where((own_row == own_col) & (own_col < count), 0.01, 0.0)
        for j in range(0, count - 1, 2):
            if j == count // 2 - 1:
                middle()
            first_col = jnp.broadcast_to(system[:, j:j + 1], (32, LANES))
            second_col = jnp.broadcast_to(system[:, j + 1:j + 2], (32, LANES))
            first_row, second_row = system[j:j + 1, :], system[j + 1:j + 2, :]
            a, b = first_col[j:j + 1, :], second_col[j:j + 1, :]
            c, d = first_col[j + 1:j + 2, :], second_col[j + 1:j + 2, :]
            inverse = 1.0 / (a * d - b * c)
            first = (d * first_row - b * second_row) * inverse
            second = (a * second_row - c * first_row) * inverse
            rest = system - first_col * first - second_col * second
            system = jnp.where(own_row == j, first, jnp.where(own_row == j + 1, second, rest))
        last = count - 1
        pivot_col = jnp.broadcast_to(system[:, last:last + 1], (32, LANES))
        scaled = system[last:last + 1, :] * (1.0 / pivot_col[last:last + 1, :])
        system = jnp.where(own_row == last, scaled, system - pivot_col * scaled)
        cs[...] = jnp.broadcast_to(system[:, count:count + 1], (32, LANES))

    def spread_copy(d, hop, slot, part):
        source = dt.at[slot, part_rows(part)] if hop == 0 else dbank.at[d, hop - 1, slot, part_rows(part)]
        return remote(source, dbank.at[d, hop, slot, part_rows(part)],
                      ds_.at[d, hop, slot, part], dr.at[d, hop, slot, part], ahead[d])

    def subtract(slot):
        for part in range(CHUNKS):
            for g in range(groups):
                sl = group(part, g)
                total = sci[slot, sl, :]
                for k in range(count):
                    weight = jnp.broadcast_to(cs[k:k + 1, :], (8, LANES))
                    total = total - jnp.concatenate([weight] * blocks, axis=1) * img[k, sl, :]
                diff[slot, sl, :] = total
                dt[slot, sl, :] = pltpu.roll(total, offs[slot], 1)
            for d in range(2):
                spread_copy(d, 0, slot, part).start()

    def forward(hop, slot, part):
        for d in range(2):
            spread_copy(d, hop, slot, part).wait_recv()
            if hop + 1 < REACH:
                spread_copy(d, hop + 1, slot, part).start()

    def add(step, slot, data, parts=range(CHUNKS)):
        wanted = owner(step, slot)
        for part in parts:
            for g in range(groups):
                value = data[group(part, g), :]
                for t in range(slots):
                    coadd[t, group(part, g), :] += jnp.where(wanted == slots * me + t, value, 0.0)

    def nothing():
        pass

    for part in range(CHUNKS):
        relay(0, 0, part)
    bands(0, 16)
    for part in range(CHUNKS):
        relay(1, 0, part)
    bands(16, 24)
    for part in range(CHUNKS):
        relay(2, 0, part)
    for part in range(CHUNKS):
        relay(0, 1, part)
    bands(24, count)
    for t in range(slots):
        coadd[t] = jnp.zeros((rows, cols), F32)

    assemble(0)
    relay(1, 1, 0)
    relay(1, 1, 1)
    edges(0)
    row_step()
    relay(1, 1, 2)
    column_step(0)
    column_step(1)
    relay(2, 1, 0)
    column_step(2)
    relay(2, 1, 1)
    column_step(3)
    products(0)
    relay(2, 1, 2)
    solve(0, nothing)
    subtract(0)
    assemble(1)
    add(0, 0, dt.at[0])

    edges(1)
    row_step()
    column_step(0)
    column_step(1)
    column_step(2)
    forward(0, 0, 0)
    column_step(3)
    forward(0, 0, 1)
    products(1)
    forward(0, 0, 2)
    forward(1, 0, 0)
    forward(1, 0, 1)
    solve(1, functools.partial(forward, 1, 0, 2))
    subtract(1)

    add(0, 1, dt.at[1])
    for d, sign in enumerate(SIGN):
        add(-sign, 0, dbank.at[d, 0, 0])
    for part in range(CHUNKS):
        forward(0, 1, part)
    for d, sign in enumerate(SIGN):
        add(-2 * sign, 0, dbank.at[d, 1, 0])
    for part in range(CHUNKS):
        forward(1, 1, part)
    for part in range(CHUNKS):
        forward(2, 0, part)
    for d, sign in enumerate(SIGN):
        add(-3 * sign, 0, dbank.at[d, 2, 0])
        add(-sign, 1, dbank.at[d, 0, 1])
        add(-2 * sign, 1, dbank.at[d, 1, 1])
    for part in range(CHUNKS):
        forward(2, 1, part)
        for d, sign in enumerate(SIGN):
            add(-3 * sign, 1, dbank.at[d, 2, 1], (part,))

    for slot in range(slots):
        down, up = halo_copies(slot)

        @pl.when(q < nq - 1)
        def _():
            down.wait_send()

        @pl.when(q > 0)
        def _():
            up.wait_send()

        for copy in gram_copies(slot):
            copy.wait_send()
        for part in range(CHUNKS):
            for d in range(2):
                for hop in range(REACH):
                    hop_copy(d, hop + 1, slot, part).wait_send()
                    spread_copy(d, hop, slot, part).wait_send()


def on_device(science, reference_tiles, visit_tiles, offsets, basis_rows, basis_cols):
    slots, rows, cols = science.shape
    count = basis_rows.shape[0]
    nq = lax.axis_size("quad")
    pixels = nq * rows * cols
    pad = ((0, 32 - count), (0, LANES - basis_rows.shape[1]))
    brow = jnp.pad(basis_rows, pad)
    bcol = jnp.pad(basis_cols[:, ::-1], pad)
    vmem = pl.BlockSpec(memory_space=pltpu.VMEM)
    smem = pl.BlockSpec(memory_space=pltpu.SMEM)
    dma = pltpu.SemaphoreType.DMA
    ext_cols = cols + 2 * LANES
    return pl.pallas_call(
        functools.partial(kernel, float(pixels)),
        out_shape=[jax.ShapeDtypeStruct((slots, rows, cols), F32)] * 2,
        in_specs=[vmem, vmem, smem, smem, vmem, vmem],
        out_specs=[vmem, vmem],
        scratch_shapes=[
            pltpu.VMEM((2 * REACH + 1, 8, LANES), jnp.int32),
            pltpu.VMEM((REACH + 1, 2, slots, rows, cols), F32),
            pltpu.VMEM((slots, rows, cols), F32),
            pltpu.VMEM((slots, 2, HALO, cols), F32),
            pltpu.VMEM((256, ext_cols), BF16),
            pltpu.VMEM((count * rows, 256), BF16),
            pltpu.VMEM((3, 32, 256), F32),
            pltpu.VMEM((count, 256, 256), BF16),
            pltpu.VMEM((count * rows, ext_cols), BF16),
            pltpu.VMEM((count * rows, ext_cols), BF16),
            pltpu.VMEM((count + 1, rows, cols), F32),
            pltpu.VMEM((256, 512), F32),
            pltpu.VMEM((slots, nq, 32, LANES), F32),
            pltpu.VMEM((32, LANES), F32),
            pltpu.VMEM((slots, rows, cols), F32),
            pltpu.VMEM((2, REACH, slots, rows, cols), F32),
            dma((2 * REACH + 1,)), dma((2 * REACH + 1,)),
            dma((REACH, 2, slots, CHUNKS)), dma((REACH, 2, slots, CHUNKS)),
            dma((slots, 2)), dma((slots, 2)),
            dma((slots, nq - 1)), dma((slots, nq - 1)),
            dma((2, REACH, slots, CHUNKS)), dma((2, REACH, slots, CHUNKS)),
        ],
        compiler_params=pltpu.CompilerParams(
            collective_id=0, has_side_effects=True, vmem_limit_bytes=56 * 1024 * 1024
        ),
        cost_estimate=pl.CostEstimate(flops=8_000_000_000, bytes_accessed=2_000_000, transcendentals=0),
    )(science, reference_tiles, visit_tiles, offsets, brow, bcol)


def solution(mesh):
    tiles = P("visit", "quad", None)
    return jax.shard_map(
        on_device,
        mesh=mesh,
        in_specs=(tiles, tiles, P("visit", None), P("visit"), P(), P()),
        out_specs=(tiles, tiles),
        check_vma=False,
    )
```

```python
import functools

import jax
import jax.numpy as jnp
from jax import lax
from jax.experimental import pallas as pl
from jax.experimental.pallas import tpu as pltpu
from jax.sharding import PartitionSpec as P

MESH = pl.DeviceIdType.MESH
REACH = 3
LANES = 128
HALO = 16
CHUNKS = 3
EXT = 80
HIGHEST = lax.Precision.HIGHEST
F32 = jnp.float32
BF16 = jnp.bfloat16
SIGN = (1, -1)


def split(x):
    high = x.astype(BF16)
    return high, (x - high.astype(F32)).astype(BF16)


def kernel(
    pixels,
    sci, tiles, pairs, offs, brow, bcol,
    diff, coadd,
    metas, bank, pre, halo, tst, rmat, base, bmat, yhi, ylo, img,
    gacc, gbuf, cs, dt, dbank,
    ms, mr, ts, tr, hs, hr, gs, gr, ds_, dr,
):
    slots, rows, cols = sci.shape
    taps = 31
    count = 31
    chunk_rows = rows // CHUNKS
    nv, nq = lax.axis_size("visit"), lax.axis_size("quad")
    me, q = lax.axis_index("visit"), lax.axis_index("quad")
    blocks = cols // LANES
    groups = chunk_rows // 8

    def at_visit(step):
        return lax.rem(me + step + nv, nv)

    def at_quad(step):
        return lax.rem(q + step, nq)

    def remote(src, dst, send, recv, device):
        return pltpu.make_async_remote_copy(
            src_ref=src, dst_ref=dst, send_sem=send, recv_sem=recv,
            device_id=device, device_id_type=MESH,
        )

    steps = [step * sign for step in range(1, REACH + 1) for sign in SIGN]
    barrier = pltpu.get_barrier_semaphore()
    for step in steps:
        pl.semaphore_signal(barrier, inc=1, device_id={"visit": at_visit(step)}, device_id_type=MESH)
    for step in range(1, nq):
        pl.semaphore_signal(barrier, inc=1, device_id={"quad": at_quad(step)}, device_id_type=MESH)

    line = lax.broadcasted_iota(jnp.int32, (8, LANES), 0)
    own = jnp.zeros((8, LANES), jnp.int32)
    for slot in range(slots):
        for place, value in enumerate((pairs[slot, 0], pairs[slot, 1], offs[slot])):
            own = jnp.where(line == 3 * slot + place, value, own)
    metas[REACH] = own
    pl.semaphore_wait(barrier, len(steps) + nq - 1)

    meta_copies = [
        remote(metas.at[REACH], metas.at[REACH - step], ms.at[REACH - step], mr.at[REACH - step],
               {"visit": at_visit(step)})
        for step in steps
    ]
    for copy in meta_copies:
        copy.start()
    ahead = [{"visit": at_visit(sign)} for sign in SIGN]
    tst[...] = jnp.zeros_like(tst)
    bmat[...] = jnp.zeros_like(bmat)
    blank = jnp.zeros((32, LANES), F32)
    row_high = brow[...].astype(BF16).astype(F32)
    row_low = brow[...] - row_high
    wide_high = jnp.concatenate([row_high, blank], axis=1)
    wide_low = jnp.concatenate([row_low, blank], axis=1)
    base[0] = (
        pltpu.roll(wide_high, 1, 1) + pltpu.roll(wide_low, EXT + 1, 1) + pltpu.roll(wide_high, 2 * EXT + 1, 1)
    )
    col_high = bcol[...].astype(BF16).astype(F32)
    back = 2 * LANES - (taps - 1)
    base[1] = pltpu.roll(jnp.concatenate([col_high, blank], axis=1), back, 1)
    base[2] = pltpu.roll(jnp.concatenate([bcol[...] - col_high, blank], axis=1), back, 1)

    @pl.loop(0, count)
    def _(k):
        line_k = jnp.broadcast_to(base[0, pl.ds(k, 1), :], (rows, 2 * LANES))
        line_k = pltpu.roll(line_k, 0, 1, stride=1, stride_axis=0).astype(BF16)
        for part in range(CHUNKS):
            first = pl.multiple_of(part * count * chunk_rows + k * chunk_rows, 16)
            rmat[pl.ds(first, chunk_rows), :] = line_k[part * chunk_rows:(part + 1) * chunk_rows]

    def bands(first, last):
        @pl.loop(first, last)
        def _(k):
            for part in range(2):
                line_k = jnp.broadcast_to(base[1 + part, pl.ds(k, 1), :], (EXT, 2 * LANES))
                band = pltpu.roll(line_k, 0, 1, stride=1, stride_axis=0)
                for piece in range(2):
                    if piece:
                        band = pltpu.roll(band, EXT, 1)
                    bmat[k, piece * EXT:(piece + 1) * EXT, part * LANES:(part + 1) * LANES] = (
                        band[:, :LANES].astype(BF16)
                    )

    @pl.when(q == 0)
    def _():
        for slot in range(slots):
            halo[slot, 0] = jnp.zeros((HALO, cols), F32)

    @pl.when(q == nq - 1)
    def _():
        for slot in range(slots):
            halo[slot, 1] = jnp.zeros((HALO, cols), F32)

    for copy in meta_copies:
        copy.wait()

    column = lax.broadcasted_iota(jnp.int32, (8, cols), 1)

    def owner(step, slot):
        def wide(place):
            value = metas[REACH + step, 3 * slot + place:3 * slot + place + 1, :]
            return jnp.concatenate([jnp.broadcast_to(value, (8, LANES))] * blocks, axis=1)
        return jnp.where(column >= wide(2), wide(0), wide(1))

    def group(part, g):
        return pl.ds(part * chunk_rows + g * 8, 8)

    def part_rows(part):
        return pl.ds(part * chunk_rows, chunk_rows)

    def hop_copy(d, hop, slot, part):
        return remote(bank.at[hop - 1, d, slot, part_rows(part)], bank.at[hop, d, slot, part_rows(part)],
                      ts.at[hop - 1, d, slot, part], tr.at[hop - 1, d, slot, part], ahead[d])

    def relay(hop, slot, part):
        for d, sign in enumerate(SIGN):
            wanted = owner((REACH - hop) * sign, slot)
            if hop:
                hop_copy(d, hop, slot, part).wait_recv()
            for g in range(groups):
                sl = group(part, g)
                total = bank[hop, d, slot, sl, :] if hop else jnp.zeros((8, cols), F32)
                for t in range(slots):
                    total = jnp.where(wanted == slots * me + t, tiles[t, sl, :], total)
                bank[hop, d, slot, sl, :] = total
            hop_copy(d, hop + 1, slot, part).start()

    def halo_copies(slot):
        down = remote(pre.at[slot, pl.ds(rows - HALO, HALO)], halo.at[slot, 0],
                      hs.at[slot, 0], hr.at[slot, 0], {"quad": at_quad(1)})
        up = remote(pre.at[slot, pl.ds(0, HALO)], halo.at[slot, 1],
                    hs.at[slot, 1], hr.at[slot, 1], {"quad": at_quad(nq - 1)})
        return down, up

    lane = lax.broadcasted_iota(jnp.int32, (HALO, LANES), 1)

    def spread(x, slot, first):
        shift = lax.rem(cols + taps // 2 - offs[slot], cols)
        x = pltpu.roll(x, shift, 1)
        head = x[:, :LANES]
        ext = jnp.concatenate(
            [jnp.where(lane >= taps // 2, head, 0.0), x[:, LANES:], jnp.where(lane < taps // 2, head, 0.0)],
            axis=1,
        )
        high, low = split(ext)
        width = cols + LANES
        tst[first:first + HALO, :width] = high
        tst[EXT + first:EXT + first + HALO, :width] = high
        tst[2 * EXT + first:2 * EXT + first + HALO, :width] = low

    own_row = lax.broadcasted_iota(jnp.int32, (32, LANES), 0)
    own_col = lax.broadcasted_iota(jnp.int32, (32, LANES), 1)

    def gram_copies(slot):
        return [
            remote(gbuf.at[slot, 0], gbuf.at[slot, step], gs.at[slot, step - 1], gr.at[slot, step - 1],
                   {"quad": at_quad(step)})
            for step in range(1, nq)
        ]

    def assemble(slot):
        for part in range(CHUNKS):
            for d in range(2):
                hop_copy(d, REACH, slot, part).wait_recv()
        img[count] = sci[slot]
        gacc[...] = jnp.zeros_like(gacc)
        wanted = owner(0, slot)
        for g in range(rows // 8):
            sl = pl.ds(g * 8, 8)
            total = bank[REACH, 0, slot, sl, :] + bank[REACH, 1, slot, sl, :]
            for t in range(slots):
                total = jnp.where(wanted == slots * me + t, tiles[t, sl, :], total)
            pre[slot, sl, :] = total
        down, up = halo_copies(slot)

        @pl.when(q < nq - 1)
        def _():
            down.start()

        @pl.when(q > 0)
        def _():
            up.start()

        for g in range(rows // HALO):
            spread(pre[slot, g * HALO:(g + 1) * HALO, :], slot, HALO + g * HALO)

    def edges(slot):
        down, up = halo_copies(slot)

        @pl.when(q > 0)
        def _():
            down.wait_recv()

        @pl.when(q < nq - 1)
        def _():
            up.wait_recv()

        spread(halo[slot, 0], slot, 0)
        spread(halo[slot, 1], slot, HALO + rows)

    def row_step(parts):
        chunk = count * chunk_rows

        @pl.loop(0, (cols + 2 * LANES) // (2 * LANES), unroll=True)
        def _(n):
            sl = pl.ds(pl.multiple_of(n * 2 * LANES, 2 * LANES), 2 * LANES)
            weight = tst[:, sl]
            for part in parts:
                rsl = pl.ds(part * chunk, chunk)
                high, low = split(jnp.dot(rmat[rsl, :], weight, preferred_element_type=F32))
                yhi[rsl, sl] = high
                ylo[rsl, sl] = low

    def column_step(begin, end, parts):
        @pl.loop(begin, end, unroll=True)
        def _(k):
            left = []
            for y in (yhi, ylo):
                for part in parts:
                    first = pl.multiple_of(part * count * chunk_rows + k * chunk_rows, 16)
                    for n in range(blocks):
                        left.append(y[pl.ds(first, chunk_rows), n * LANES:(n + 2) * LANES])
            out = jnp.dot(jnp.concatenate(left, axis=0), bmat[k], preferred_element_type=F32)
            out = out[:, :LANES] + out[:, LANES:]
            size = len(parts) * blocks * chunk_rows
            out = out[:size] + out[size:]
            for place, part in enumerate(parts):
                for n in range(blocks):
                    first = (place * blocks + n) * chunk_rows
                    img[k, part * chunk_rows:(part + 1) * chunk_rows, n * LANES:(n + 1) * LANES] = (
                        out[first:first + chunk_rows]
                    )

    def products(slot, parts):
        for part in parts:
            for g in range(groups):
                x = img[:, part * chunk_rows + g * 8:part * chunk_rows + (g + 1) * 8, :].reshape(256, cols)
                high, low = split(x)
                gacc[:, :256] += lax.dot_general(high, high, (((1,), (1,)), ((), ())), preferred_element_type=F32)
                gacc[:, 256:] += lax.dot_general(high, low, (((1,), (1,)), ((), ())), preferred_element_type=F32)

    def send_products(slot):
        srow = lax.broadcasted_iota(jnp.int32, (256, 256), 0)
        scol = lax.broadcasted_iota(jnp.int32, (256, 256), 1)
        same = lax.rem(srow, 8) == lax.rem(scol, 8)
        prow = lax.broadcasted_iota(jnp.int32, (256, LANES), 0)
        pcol = lax.broadcasted_iota(jnp.int32, (256, LANES), 1)
        gather = (lax.div(prow, 8) == pcol).astype(F32)

        def reduced(x):
            x = jnp.where(same, x, 0.0).reshape(32, 8, 256).sum(axis=1)
            return jnp.dot(x, gather, precision=HIGHEST, preferred_element_type=F32)

        main = reduced(gacc[:, :256])
        cross = reduced(gacc[:, 256:])
        square = jnp.concatenate([cross, jnp.zeros((96, LANES), F32)], axis=0)
        gbuf[slot, 0] = main + cross + square.T[:32]
        for copy in gram_copies(slot):
            copy.start()

    def solve(slot, middle):
        for copy in gram_copies(slot):
            copy.wait_recv()
        total = gbuf[slot, lax.rem(q + nq, nq)]
        for source in range(1, nq):
            total = total + gbuf[slot, lax.rem(q + nq - source, nq)]
        system = total / pixels + jnp.where((own_row == own_col) & (own_col < count), 0.01, 0.0)
        for j in range(0, count - 1, 2):
            if j == count // 2 - 1:
                middle()
            first_col = jnp.broadcast_to(system[:, j:j + 1], (32, LANES))
            second_col = jnp.broadcast_to(system[:, j + 1:j + 2], (32, LANES))
            first_row, second_row = system[j:j + 1, :], system[j + 1:j + 2, :]
            a, b = first_col[j:j + 1, :], second_col[j:j + 1, :]
            c, d = first_col[j + 1:j + 2, :], second_col[j + 1:j + 2, :]
            inverse = 1.0 / (a * d - b * c)
            first = (d * first_row - b * second_row) * inverse
            second = (a * second_row - c * first_row) * inverse
            rest = system - first_col * first - second_col * second
            system = jnp.where(own_row == j, first, jnp.where(own_row == j + 1, second, rest))
        last = count - 1
        pivot_col = jnp.broadcast_to(system[:, last:last + 1], (32, LANES))
        scaled = system[last:last + 1, :] * (1.0 / pivot_col[last:last + 1, :])
        system = jnp.where(own_row == last, scaled, system - pivot_col * scaled)
        cs[...] = jnp.broadcast_to(system[:, count:count + 1], (32, LANES))

    def spread_copy(d, hop, slot, part):
        source = dt.at[slot, part_rows(part)] if hop == 0 else dbank.at[d, hop - 1, slot, part_rows(part)]
        return remote(source, dbank.at[d, hop, slot, part_rows(part)],
                      ds_.at[d, hop, slot, part], dr.at[d, hop, slot, part], ahead[d])

    def subtract(slot):
        for part in range(CHUNKS):
            for g in range(groups):
                sl = group(part, g)
                total = sci[slot, sl, :]
                for k in range(count):
                    weight = jnp.broadcast_to(cs[k:k + 1, :], (8, LANES))
                    total = total - jnp.concatenate([weight] * blocks, axis=1) * img[k, sl, :]
                diff[slot, sl, :] = total
                dt[slot, sl, :] = pltpu.roll(total, offs[slot], 1)
            for d in range(2):
                spread_copy(d, 0, slot, part).start()

    def forward(hop, slot, part):
        for d in range(2):
            spread_copy(d, hop, slot, part).wait_recv()
            if hop + 1 < REACH:
                spread_copy(d, hop + 1, slot, part).start()

    def add(step, slot, data, parts=range(CHUNKS)):
        wanted = owner(step, slot)
        for part in parts:
            for g in range(groups):
                value = data[group(part, g), :]
                for t in range(slots):
                    coadd[t, group(part, g), :] += jnp.where(wanted == slots * me + t, value, 0.0)

    def nothing():
        pass

    for part in range(CHUNKS):
        relay(0, 0, part)
    bands(0, 16)
    for part in range(CHUNKS):
        relay(1, 0, part)
    bands(16, 24)
    for part in range(CHUNKS):
        relay(2, 0, part)
    for part in range(CHUNKS):
        relay(0, 1, part)
    bands(24, count)
    for t in range(slots):
        coadd[t] = jnp.zeros((rows, cols), F32)

    inner, outer = (1,), (0, 2)
    assemble(0)
    relay(1, 1, 0)
    row_step(inner)
    relay(1, 1, 1)
    column_step(0, count, inner)
    relay(1, 1, 2)
    products(0, inner)
    edges(0)
    row_step(outer)
    column_step(0, 16, outer)
    relay(2, 1, 0)
    column_step(16, count, outer)
    relay(2, 1, 1)
    products(0, outer)
    send_products(0)
    relay(2, 1, 2)
    solve(0, nothing)
    subtract(0)

    assemble(1)
    row_step(inner)
    column_step(0, count, inner)
    products(1, inner)
    edges(1)
    row_step(outer)
    forward(0, 0, 0)
    column_step(0, 16, outer)
    forward(0, 0, 1)
    column_step(16, count, outer)
    forward(0, 0, 2)
    products(1, outer)
    send_products(1)
    add(0, 0, dt.at[0])
    forward(1, 0, 0)
    forward(1, 0, 1)
    solve(1, functools.partial(forward, 1, 0, 2))
    subtract(1)

    add(0, 1, dt.at[1])
    for d, sign in enumerate(SIGN):
        add(-sign, 0, dbank.at[d, 0, 0])
    for part in range(CHUNKS):
        forward(0, 1, part)
    for d, sign in enumerate(SIGN):
        add(-2 * sign, 0, dbank.at[d, 1, 0])
    for part in range(CHUNKS):
        forward(1, 1, part)
    for part in range(CHUNKS):
        forward(2, 0, part)
    for d, sign in enumerate(SIGN):
        add(-3 * sign, 0, dbank.at[d, 2, 0])
        add(-sign, 1, dbank.at[d, 0, 1])
        add(-2 * sign, 1, dbank.at[d, 1, 1])
    for part in range(CHUNKS):
        forward(2, 1, part)
        for d, sign in enumerate(SIGN):
            add(-3 * sign, 1, dbank.at[d, 2, 1], (part,))

    for slot in range(slots):
        down, up = halo_copies(slot)

        @pl.when(q < nq - 1)
        def _():
            down.wait_send()

        @pl.when(q > 0)
        def _():
            up.wait_send()

        for copy in gram_copies(slot):
            copy.wait_send()
        for part in range(CHUNKS):
            for d in range(2):
                for hop in range(REACH):
                    hop_copy(d, hop + 1, slot, part).wait_send()
                    spread_copy(d, hop, slot, part).wait_send()


def on_device(science, reference_tiles, visit_tiles, offsets, basis_rows, basis_cols):
    slots, rows, cols = science.shape
    count = basis_rows.shape[0]
    nq = lax.axis_size("quad")
    pixels = nq * rows * cols
    pad = ((0, 32 - count), (0, LANES - basis_rows.shape[1]))
    brow = jnp.pad(basis_rows, pad)
    bcol = jnp.pad(basis_cols[:, ::-1], pad)
    vmem = pl.BlockSpec(memory_space=pltpu.VMEM)
    smem = pl.BlockSpec(memory_space=pltpu.SMEM)
    dma = pltpu.SemaphoreType.DMA
    ext_cols = cols + 2 * LANES
    return pl.pallas_call(
        functools.partial(kernel, float(pixels)),
        out_shape=[jax.ShapeDtypeStruct((slots, rows, cols), F32)] * 2,
        in_specs=[vmem, vmem, smem, smem, vmem, vmem],
        out_specs=[vmem, vmem],
        scratch_shapes=[
            pltpu.VMEM((2 * REACH + 1, 8, LANES), jnp.int32),
            pltpu.VMEM((REACH + 1, 2, slots, rows, cols), F32),
            pltpu.VMEM((slots, rows, cols), F32),
            pltpu.VMEM((slots, 2, HALO, cols), F32),
            pltpu.VMEM((256, ext_cols), BF16),
            pltpu.VMEM((count * rows, 256), BF16),
            pltpu.VMEM((3, 32, 256), F32),
            pltpu.VMEM((count, 256, 256), BF16),
            pltpu.VMEM((count * rows, ext_cols), BF16),
            pltpu.VMEM((count * rows, ext_cols), BF16),
            pltpu.VMEM((count + 1, rows, cols), F32),
            pltpu.VMEM((256, 512), F32),
            pltpu.VMEM((slots, nq, 32, LANES), F32),
            pltpu.VMEM((32, LANES), F32),
            pltpu.VMEM((slots, rows, cols), F32),
            pltpu.VMEM((2, REACH, slots, rows, cols), F32),
            dma((2 * REACH + 1,)), dma((2 * REACH + 1,)),
            dma((REACH, 2, slots, CHUNKS)), dma((REACH, 2, slots, CHUNKS)),
            dma((slots, 2)), dma((slots, 2)),
            dma((slots, nq - 1)), dma((slots, nq - 1)),
            dma((2, REACH, slots, CHUNKS)), dma((2, REACH, slots, CHUNKS)),
        ],
        compiler_params=pltpu.CompilerParams(
            collective_id=0, has_side_effects=True, vmem_limit_bytes=56 * 1024 * 1024
        ),
        cost_estimate=pl.CostEstimate(flops=8_000_000_000, bytes_accessed=2_000_000, transcendentals=0),
    )(science, reference_tiles, visit_tiles, offsets, brow, bcol)


def solution(mesh):
    tiles = P("visit", "quad", None)
    return jax.shard_map(
        on_device,
        mesh=mesh,
        in_specs=(tiles, tiles, P("visit", None), P("visit"), P(), P()),
        out_specs=(tiles, tiles),
        check_vma=False,
    )
```

```python
import functools

import jax
import jax.numpy as jnp
from jax import lax
from jax.experimental import pallas as pl
from jax.experimental.pallas import tpu as pltpu
from jax.sharding import PartitionSpec as P

MESH = pl.DeviceIdType.MESH
REACH = 3
LANES = 128
HALO = 16
CHUNKS = 6
EXT = 80
HIGHEST = lax.Precision.HIGHEST
F32 = jnp.float32
BF16 = jnp.bfloat16
SIGN = (1, -1)


def split(x):
    high = x.astype(BF16)
    return high, (x - high.astype(F32)).astype(BF16)


def kernel(
    pixels,
    sci, tiles, pairs, offs, brow, bcol,
    diff, coadd,
    metas, bank, pre, halo, tst, rmat, base, bmat, yhi, ylo, img,
    gacc, gbuf, cs, dt, dbank,
    ms, mr, ts, tr, hs, hr, gs, gr, ds_, dr,
):
    slots, rows, cols = sci.shape
    taps = 31
    count = 31
    chunk_rows = rows // CHUNKS
    nv, nq = lax.axis_size("visit"), lax.axis_size("quad")
    me, q = lax.axis_index("visit"), lax.axis_index("quad")
    blocks = cols // LANES
    groups = chunk_rows // 8

    def at_visit(step):
        return lax.rem(me + step + nv, nv)

    def at_quad(step):
        return lax.rem(q + step, nq)

    def remote(src, dst, send, recv, device):
        return pltpu.make_async_remote_copy(
            src_ref=src, dst_ref=dst, send_sem=send, recv_sem=recv,
            device_id=device, device_id_type=MESH,
        )

    steps = [step * sign for step in range(1, REACH + 1) for sign in SIGN]
    barrier = pltpu.get_barrier_semaphore()
    for step in steps:
        pl.semaphore_signal(barrier, inc=1, device_id={"visit": at_visit(step)}, device_id_type=MESH)
    for step in range(1, nq):
        pl.semaphore_signal(barrier, inc=1, device_id={"quad": at_quad(step)}, device_id_type=MESH)

    line = lax.broadcasted_iota(jnp.int32, (8, LANES), 0)
    own = jnp.zeros((8, LANES), jnp.int32)
    for slot in range(slots):
        for place, value in enumerate((pairs[slot, 0], pairs[slot, 1], offs[slot])):
            own = jnp.where(line == 3 * slot + place, value, own)
    metas[REACH] = own
    pl.semaphore_wait(barrier, len(steps) + nq - 1)

    meta_copies = [
        remote(metas.at[REACH], metas.at[REACH - step], ms.at[REACH - step], mr.at[REACH - step],
               {"visit": at_visit(step)})
        for step in steps
    ]
    for copy in meta_copies:
        copy.start()
    ahead = [{"visit": at_visit(sign)} for sign in SIGN]
    tst[...] = jnp.zeros_like(tst)
    bmat[...] = jnp.zeros_like(bmat)
    blank = jnp.zeros((32, LANES), F32)
    row_high = brow[...].astype(BF16).astype(F32)
    row_low = brow[...] - row_high
    wide_high = jnp.concatenate([row_high, blank], axis=1)
    wide_low = jnp.concatenate([row_low, blank], axis=1)
    base[0] = (
        pltpu.roll(wide_high, 1, 1) + pltpu.roll(wide_low, EXT + 1, 1) + pltpu.roll(wide_high, 2 * EXT + 1, 1)
    )
    col_high = bcol[...].astype(BF16).astype(F32)
    back = 2 * LANES - (taps - 1)
    base[1] = pltpu.roll(jnp.concatenate([col_high, blank], axis=1), back, 1)
    base[2] = pltpu.roll(jnp.concatenate([bcol[...] - col_high, blank], axis=1), back, 1)

    @pl.loop(0, count)
    def _(k):
        first = pl.multiple_of(k * rows, 16)
        line_k = jnp.broadcast_to(base[0, pl.ds(k, 1), :], (rows, 2 * LANES))
        rmat[pl.ds(first, rows), :] = pltpu.roll(line_k, 0, 1, stride=1, stride_axis=0).astype(BF16)

    def bands(first, last):
        @pl.loop(first, last)
        def _(k):
            for part in range(2):
                line_k = jnp.broadcast_to(base[1 + part, pl.ds(k, 1), :], (EXT, 2 * LANES))
                band = pltpu.roll(line_k, 0, 1, stride=1, stride_axis=0)
                for piece in range(2):
                    if piece:
                        band = pltpu.roll(band, EXT, 1)
                    bmat[k, piece * EXT:(piece + 1) * EXT, part * LANES:(part + 1) * LANES] = (
                        band[:, :LANES].astype(BF16)
                    )

    @pl.when(q == 0)
    def _():
        for slot in range(slots):
            halo[slot, 0] = jnp.zeros((HALO, cols), F32)

    @pl.when(q == nq - 1)
    def _():
        for slot in range(slots):
            halo[slot, 1] = jnp.zeros((HALO, cols), F32)

    for copy in meta_copies:
        copy.wait()

    column = lax.broadcasted_iota(jnp.int32, (8, cols), 1)

    def owner(step, slot):
        def wide(place):
            value = metas[REACH + step, 3 * slot + place:3 * slot + place + 1, :]
            return jnp.concatenate([jnp.broadcast_to(value, (8, LANES))] * blocks, axis=1)
        return jnp.where(column >= wide(2), wide(0), wide(1))

    def group(part, g):
        return pl.ds(part * chunk_rows + g * 8, 8)

    def part_rows(part):
        return pl.ds(part * chunk_rows, chunk_rows)

    def hop_copy(d, hop, slot, part):
        return remote(bank.at[hop - 1, d, slot, part_rows(part)], bank.at[hop, d, slot, part_rows(part)],
                      ts.at[hop - 1, d, slot, part], tr.at[hop - 1, d, slot, part], ahead[d])

    def relay(hop, slot, part):
        for d, sign in enumerate(SIGN):
            wanted = owner((REACH - hop) * sign, slot)
            if hop:
                hop_copy(d, hop, slot, part).wait_recv()
            for g in range(groups):
                sl = group(part, g)
                total = bank[hop, d, slot, sl, :] if hop else jnp.zeros((8, cols), F32)
                for t in range(slots):
                    total = jnp.where(wanted == slots * me + t, tiles[t, sl, :], total)
                bank[hop, d, slot, sl, :] = total
            hop_copy(d, hop + 1, slot, part).start()

    def halo_copies(slot):
        down = remote(pre.at[slot, pl.ds(rows - HALO, HALO)], halo.at[slot, 0],
                      hs.at[slot, 0], hr.at[slot, 0], {"quad": at_quad(1)})
        up = remote(pre.at[slot, pl.ds(0, HALO)], halo.at[slot, 1],
                    hs.at[slot, 1], hr.at[slot, 1], {"quad": at_quad(nq - 1)})
        return down, up

    lane = lax.broadcasted_iota(jnp.int32, (HALO, LANES), 1)

    def spread(x, slot, first):
        shift = lax.rem(cols + taps // 2 - offs[slot], cols)
        x = pltpu.roll(x, shift, 1)
        head = x[:, :LANES]
        ext = jnp.concatenate(
            [jnp.where(lane >= taps // 2, head, 0.0), x[:, LANES:], jnp.where(lane < taps // 2, head, 0.0)],
            axis=1,
        )
        high, low = split(ext)
        width = cols + LANES
        tst[first:first + HALO, :width] = high
        tst[EXT + first:EXT + first + HALO, :width] = high
        tst[2 * EXT + first:2 * EXT + first + HALO, :width] = low

    own_row = lax.broadcasted_iota(jnp.int32, (32, LANES), 0)
    own_col = lax.broadcasted_iota(jnp.int32, (32, LANES), 1)

    def gram_copies(slot):
        return [
            remote(gbuf.at[slot, 0], gbuf.at[slot, step], gs.at[slot, step - 1], gr.at[slot, step - 1],
                   {"quad": at_quad(step)})
            for step in range(1, nq)
        ]

    def assemble(slot):
        for part in range(CHUNKS):
            for d in range(2):
                hop_copy(d, REACH, slot, part).wait_recv()
        wanted = owner(0, slot)
        for g in range(rows // 8):
            sl = pl.ds(g * 8, 8)
            total = bank[REACH, 0, slot, sl, :] + bank[REACH, 1, slot, sl, :]
            for t in range(slots):
                total = jnp.where(wanted == slots * me + t, tiles[t, sl, :], total)
            pre[slot, sl, :] = total
        down, up = halo_copies(slot)

        @pl.when(q < nq - 1)
        def _():
            down.start()

        @pl.when(q > 0)
        def _():
            up.start()

        for g in range(rows // HALO):
            spread(pre[slot, g * HALO:(g + 1) * HALO, :], slot, HALO + g * HALO)

    def edges(slot):
        down, up = halo_copies(slot)

        @pl.when(q > 0)
        def _():
            down.wait_recv()

        @pl.when(q < nq - 1)
        def _():
            up.wait_recv()

        spread(halo[slot, 0], slot, 0)
        spread(halo[slot, 1], slot, HALO + rows)

    def row_step():
        chunk = count * HALO

        @pl.loop(0, (cols + 2 * LANES) // (2 * LANES), unroll=True)
        def _(n):
            sl = pl.ds(pl.multiple_of(n * 2 * LANES, 2 * LANES), 2 * LANES)
            weight = tst[:, sl]
            for piece in range(count * rows // chunk):
                rsl = pl.ds(piece * chunk, chunk)
                high, low = split(jnp.dot(rmat[rsl, :], weight, preferred_element_type=F32))
                yhi[rsl, sl] = high
                ylo[rsl, sl] = low

    bounds = (0, 8, 16, 24, count)

    def column_step(segment):
        @pl.loop(bounds[segment], bounds[segment + 1], unroll=True)
        def _(k):
            rsl = pl.ds(pl.multiple_of(k * rows, 16), rows)
            left = jnp.concatenate(
                [y[rsl, n * LANES:(n + 2) * LANES] for y in (yhi, ylo) for n in range(blocks)], axis=0
            )
            out = jnp.dot(left, bmat[k], preferred_element_type=F32)
            out = out[:, :LANES] + out[:, LANES:]
            out = out[:rows * blocks] + out[rows * blocks:]
            for n in range(blocks):
                img[k, :, n * LANES:(n + 1) * LANES] = out[n * rows:(n + 1) * rows]

    def products(slot):
        img[count] = sci[slot]
        gacc[...] = jnp.zeros_like(gacc)

        @pl.loop(0, rows // 8, unroll=True)
        def _(g):
            x = img[:, pl.ds(pl.multiple_of(g * 8, 8), 8), :].reshape(256, cols)
            high, low = split(x)
            gacc[:, :256] += lax.dot_general(high, high, (((1,), (1,)), ((), ())), preferred_element_type=F32)
            gacc[:, 256:] += lax.dot_general(high, low, (((1,), (1,)), ((), ())), preferred_element_type=F32)

        srow = lax.broadcasted_iota(jnp.int32, (256, 256), 0)
        scol = lax.broadcasted_iota(jnp.int32, (256, 256), 1)
        same = lax.rem(srow, 8) == lax.rem(scol, 8)
        prow = lax.broadcasted_iota(jnp.int32, (256, LANES), 0)
        pcol = lax.broadcasted_iota(jnp.int32, (256, LANES), 1)
        gather = (lax.div(prow, 8) == pcol).astype(F32)

        def reduced(x):
            x = jnp.where(same, x, 0.0).reshape(32, 8, 256).sum(axis=1)
            return jnp.dot(x, gather, precision=HIGHEST, preferred_element_type=F32)

        main = reduced(gacc[:, :256])
        cross = reduced(gacc[:, 256:])
        square = jnp.concatenate([cross, jnp.zeros((96, LANES), F32)], axis=0)
        gbuf[slot, 0] = main + cross + square.T[:32]
        for copy in gram_copies(slot):
            copy.start()

    def solve(slot, middle):
        for copy in gram_copies(slot):
            copy.wait_recv()
        total = gbuf[slot, lax.rem(q + nq, nq)]
        for source in range(1, nq):
            total = total + gbuf[slot, lax.rem(q + nq - source, nq)]
        system = total / pixels + jnp.where((own_row == own_col) & (own_col < count), 0.01, 0.0)
        for j in range(0, count - 1, 2):
            if j == count // 2 - 1:
                middle()
            first_col = jnp.broadcast_to(system[:, j:j + 1], (32, LANES))
            second_col = jnp.broadcast_to(system[:, j + 1:j + 2], (32, LANES))
            first_row, second_row = system[j:j + 1, :], system[j + 1:j + 2, :]
            a, b = first_col[j:j + 1, :], second_col[j:j + 1, :]
            c, d = first_col[j + 1:j + 2, :], second_col[j + 1:j + 2, :]
            inverse = 1.0 / (a * d - b * c)
            first = (d * first_row - b * second_row) * inverse
            second = (a * second_row - c * first_row) * inverse
            rest = system - first_col * first - second_col * second
            system = jnp.where(own_row == j, first, jnp.where(own_row == j + 1, second, rest))
        last = count - 1
        pivot_col = jnp.broadcast_to(system[:, last:last + 1], (32, LANES))
        scaled = system[last:last + 1, :] * (1.0 / pivot_col[last:last + 1, :])
        system = jnp.where(own_row == last, scaled, system - pivot_col * scaled)
        cs[...] = jnp.broadcast_to(system[:, count:count + 1], (32, LANES))

    def spread_copy(d, hop, slot, part):
        source = dt.at[slot, part_rows(part)] if hop == 0 else dbank.at[d, hop - 1, slot, part_rows(part)]
        return remote(source, dbank.at[d, hop, slot, part_rows(part)],
                      ds_.at[d, hop, slot, part], dr.at[d, hop, slot, part], ahead[d])

    def subtract(slot):
        for part in range(CHUNKS):
            for g in range(groups):
                sl = group(part, g)
                total = sci[slot, sl, :]
                for k in range(count):
                    weight = jnp.broadcast_to(cs[k:k + 1, :], (8, LANES))
                    total = total - jnp.concatenate([weight] * blocks, axis=1) * img[k, sl, :]
                diff[slot, sl, :] = total
                dt[slot, sl, :] = pltpu.roll(total, offs[slot], 1)
            for d in range(2):
                spread_copy(d, 0, slot, part).start()

    def forward(hop, slot, part):
        for d in range(2):
            spread_copy(d, hop, slot, part).wait_recv()
            if hop + 1 < REACH:
                spread_copy(d, hop + 1, slot, part).start()

    def add(step, slot, data, parts=range(CHUNKS)):
        wanted = owner(step, slot)
        for part in parts:
            for g in range(groups):
                value = data[group(part, g), :]
                for t in range(slots):
                    coadd[t, group(part, g), :] += jnp.where(wanted == slots * me + t, value, 0.0)

    def nothing():
        pass

    for part in range(CHUNKS):
        relay(0, 0, part)
    bands(0, 16)
    for part in range(CHUNKS):
        relay(1, 0, part)
    bands(16, 24)
    for part in range(CHUNKS):
        relay(2, 0, part)
    for part in range(CHUNKS):
        relay(0, 1, part)
    bands(24, count)
    for t in range(slots):
        coadd[t] = jnp.zeros((rows, cols), F32)

    def third(step, hop, slot, place):
        for part in range(place * CHUNKS // 3, (place + 1) * CHUNKS // 3):
            step(hop, slot, part)

    assemble(0)
    third(relay, 1, 1, 0)
    third(relay, 1, 1, 1)
    edges(0)
    row_step()
    third(relay, 1, 1, 2)
    column_step(0)
    column_step(1)
    third(relay, 2, 1, 0)
    column_step(2)
    third(relay, 2, 1, 1)
    column_step(3)
    products(0)
    third(relay, 2, 1, 2)
    solve(0, nothing)
    subtract(0)
    assemble(1)
    add(0, 0, dt.at[0])

    edges(1)
    row_step()
    column_step(0)
    column_step(1)
    column_step(2)
    third(forward, 0, 0, 0)
    column_step(3)
    third(forward, 0, 0, 1)
    products(1)
    third(forward, 0, 0, 2)
    third(forward, 1, 0, 0)
    third(forward, 1, 0, 1)
    solve(1, functools.partial(third, forward, 1, 0, 2))
    subtract(1)

    add(0, 1, dt.at[1])
    for d, sign in enumerate(SIGN):
        add(-sign, 0, dbank.at[d, 0, 0])
    for part in range(CHUNKS):
        forward(0, 1, part)
    for d, sign in enumerate(SIGN):
        add(-2 * sign, 0, dbank.at[d, 1, 0])
    for part in range(CHUNKS):
        forward(1, 1, part)
    for part in range(CHUNKS):
        forward(2, 0, part)
    for d, sign in enumerate(SIGN):
        add(-3 * sign, 0, dbank.at[d, 2, 0])
        add(-sign, 1, dbank.at[d, 0, 1])
        add(-2 * sign, 1, dbank.at[d, 1, 1])
    for part in range(CHUNKS):
        forward(2, 1, part)
        for d, sign in enumerate(SIGN):
            add(-3 * sign, 1, dbank.at[d, 2, 1], (part,))

    for slot in range(slots):
        down, up = halo_copies(slot)

        @pl.when(q < nq - 1)
        def _():
            down.wait_send()

        @pl.when(q > 0)
        def _():
            up.wait_send()

        for copy in gram_copies(slot):
            copy.wait_send()
        for part in range(CHUNKS):
            for d in range(2):
                for hop in range(REACH):
                    hop_copy(d, hop + 1, slot, part).wait_send()
                    spread_copy(d, hop, slot, part).wait_send()


def on_device(science, reference_tiles, visit_tiles, offsets, basis_rows, basis_cols):
    slots, rows, cols = science.shape
    count = basis_rows.shape[0]
    nq = lax.axis_size("quad")
    pixels = nq * rows * cols
    pad = ((0, 32 - count), (0, LANES - basis_rows.shape[1]))
    brow = jnp.pad(basis_rows, pad)
    bcol = jnp.pad(basis_cols[:, ::-1], pad)
    vmem = pl.BlockSpec(memory_space=pltpu.VMEM)
    smem = pl.BlockSpec(memory_space=pltpu.SMEM)
    dma = pltpu.SemaphoreType.DMA
    ext_cols = cols + 2 * LANES
    return pl.pallas_call(
        functools.partial(kernel, float(pixels)),
        out_shape=[jax.ShapeDtypeStruct((slots, rows, cols), F32)] * 2,
        in_specs=[vmem, vmem, smem, smem, vmem, vmem],
        out_specs=[vmem, vmem],
        scratch_shapes=[
            pltpu.VMEM((2 * REACH + 1, 8, LANES), jnp.int32),
            pltpu.VMEM((REACH + 1, 2, slots, rows, cols), F32),
            pltpu.VMEM((slots, rows, cols), F32),
            pltpu.VMEM((slots, 2, HALO, cols), F32),
            pltpu.VMEM((256, ext_cols), BF16),
            pltpu.VMEM((count * rows, 256), BF16),
            pltpu.VMEM((3, 32, 256), F32),
            pltpu.VMEM((count, 256, 256), BF16),
            pltpu.VMEM((count * rows, ext_cols), BF16),
            pltpu.VMEM((count * rows, ext_cols), BF16),
            pltpu.VMEM((count + 1, rows, cols), F32),
            pltpu.VMEM((256, 512), F32),
            pltpu.VMEM((slots, nq, 32, LANES), F32),
            pltpu.VMEM((32, LANES), F32),
            pltpu.VMEM((slots, rows, cols), F32),
            pltpu.VMEM((2, REACH, slots, rows, cols), F32),
            dma((2 * REACH + 1,)), dma((2 * REACH + 1,)),
            dma((REACH, 2, slots, CHUNKS)), dma((REACH, 2, slots, CHUNKS)),
            dma((slots, 2)), dma((slots, 2)),
            dma((slots, nq - 1)), dma((slots, nq - 1)),
            dma((2, REACH, slots, CHUNKS)), dma((2, REACH, slots, CHUNKS)),
        ],
        compiler_params=pltpu.CompilerParams(
            collective_id=0, has_side_effects=True, vmem_limit_bytes=56 * 1024 * 1024
        ),
        cost_estimate=pl.CostEstimate(flops=8_000_000_000, bytes_accessed=2_000_000, transcendentals=0),
    )(science, reference_tiles, visit_tiles, offsets, brow, bcol)


def solution(mesh):
    tiles = P("visit", "quad", None)
    return jax.shard_map(
        on_device,
        mesh=mesh,
        in_specs=(tiles, tiles, P("visit", None), P("visit"), P(), P()),
        out_specs=(tiles, tiles),
        check_vma=False,
    )
```

```python
import functools

import jax
import jax.numpy as jnp
from jax import lax
from jax.experimental import pallas as pl
from jax.experimental.pallas import tpu as pltpu
from jax.sharding import PartitionSpec as P

MESH = pl.DeviceIdType.MESH
REACH = 3
LANES = 128
HALO = 16
CHUNKS = 3
EXT = 80
HIGHEST = lax.Precision.HIGHEST
F32 = jnp.float32
BF16 = jnp.bfloat16
SIGN = (1, -1)


def split(x):
    high = x.astype(BF16)
    return high, (x - high.astype(F32)).astype(BF16)


def kernel(
    pixels,
    sci, tiles, pairs, offs, brow, bcol,
    diff, coadd,
    metas, bank, pre, halo, tst, rmat, base, bmat, yhi, ylo, img,
    gacc, gbuf, cs, dt, dbank,
    ms, mr, ts, tr, hs, hr, gs, gr, ds_, dr,
):
    slots, rows, cols = sci.shape
    taps = 31
    count = 31
    chunk_rows = rows // CHUNKS
    nv, nq = lax.axis_size("visit"), lax.axis_size("quad")
    me, q = lax.axis_index("visit"), lax.axis_index("quad")
    blocks = cols // LANES
    groups = chunk_rows // 8

    def at_visit(step):
        return lax.rem(me + step + nv, nv)

    def at_quad(step):
        return lax.rem(q + step, nq)

    def remote(src, dst, send, recv, device):
        return pltpu.make_async_remote_copy(
            src_ref=src, dst_ref=dst, send_sem=send, recv_sem=recv,
            device_id=device, device_id_type=MESH,
        )

    steps = [step * sign for step in range(1, REACH + 1) for sign in SIGN]
    barrier = pltpu.get_barrier_semaphore()
    for step in steps:
        pl.semaphore_signal(barrier, inc=1, device_id={"visit": at_visit(step)}, device_id_type=MESH)
    for step in range(1, nq):
        pl.semaphore_signal(barrier, inc=1, device_id={"quad": at_quad(step)}, device_id_type=MESH)

    line = lax.broadcasted_iota(jnp.int32, (8, LANES), 0)
    own = jnp.zeros((8, LANES), jnp.int32)
    for slot in range(slots):
        for place, value in enumerate((pairs[slot, 0], pairs[slot, 1], offs[slot])):
            own = jnp.where(line == 3 * slot + place, value, own)
    metas[REACH] = own
    pl.semaphore_wait(barrier, len(steps) + nq - 1)

    meta_copies = [
        remote(metas.at[REACH], metas.at[REACH - step], ms.at[REACH - step], mr.at[REACH - step],
               {"visit": at_visit(step)})
        for step in steps
    ]
    for copy in meta_copies:
        copy.start()
    ahead = [{"visit": at_visit(sign)} for sign in SIGN]
    tst[...] = jnp.zeros_like(tst)
    bmat[...] = jnp.zeros_like(bmat)
    blank = jnp.zeros((32, LANES), F32)
    row_high = brow[...].astype(BF16).astype(F32)
    row_low = brow[...] - row_high
    wide_high = jnp.concatenate([row_high, blank], axis=1)
    wide_low = jnp.concatenate([row_low, blank], axis=1)
    base[0] = (
        pltpu.roll(wide_high, 1, 1) + pltpu.roll(wide_low, EXT + 1, 1) + pltpu.roll(wide_high, 2 * EXT + 1, 1)
    )
    col_high = bcol[...].astype(BF16).astype(F32)
    back = 2 * LANES - (taps - 1)
    base[1] = pltpu.roll(jnp.concatenate([col_high, blank], axis=1), back, 1)
    base[2] = pltpu.roll(jnp.concatenate([bcol[...] - col_high, blank], axis=1), back, 1)

    @pl.loop(0, count)
    def _(k):
        first = pl.multiple_of(k * rows, 16)
        line_k = jnp.broadcast_to(base[0, pl.ds(k, 1), :], (rows, 2 * LANES))
        rmat[pl.ds(first, rows), :] = pltpu.roll(line_k, 0, 1, stride=1, stride_axis=0).astype(BF16)

    def bands(first, last):
        @pl.loop(first, last)
        def _(k):
            for part in range(2):
                line_k = jnp.broadcast_to(base[1 + part, pl.ds(k, 1), :], (EXT, 2 * LANES))
                band = pltpu.roll(line_k, 0, 1, stride=1, stride_axis=0)
                for piece in range(2):
                    if piece:
                        band = pltpu.roll(band, EXT, 1)
                    bmat[k, piece * EXT:(piece + 1) * EXT, part * LANES:(part + 1) * LANES] = (
                        band[:, :LANES].astype(BF16)
                    )

    @pl.when(q == 0)
    def _():
        for slot in range(slots):
            halo[slot, 0] = jnp.zeros((HALO, cols), F32)

    @pl.when(q == nq - 1)
    def _():
        for slot in range(slots):
            halo[slot, 1] = jnp.zeros((HALO, cols), F32)

    for copy in meta_copies:
        copy.wait()

    column = lax.broadcasted_iota(jnp.int32, (8, cols), 1)

    def owner(step, slot):
        def wide(place):
            value = metas[REACH + step, 3 * slot + place:3 * slot + place + 1, :]
            return jnp.concatenate([jnp.broadcast_to(value, (8, LANES))] * blocks, axis=1)
        return jnp.where(column >= wide(2), wide(0), wide(1))

    def group(part, g):
        return pl.ds(part * chunk_rows + g * 8, 8)

    def part_rows(part):
        return pl.ds(part * chunk_rows, chunk_rows)

    def hop_copy(d, hop, slot, part):
        return remote(bank.at[hop - 1, d, slot, part_rows(part)], bank.at[hop, d, slot, part_rows(part)],
                      ts.at[hop - 1, d, slot, part], tr.at[hop - 1, d, slot, part], ahead[d])

    def relay(hop, slot, part):
        for d, sign in enumerate(SIGN):
            wanted = owner((REACH - hop) * sign, slot)
            if hop:
                hop_copy(d, hop, slot, part).wait_recv()
            for g in range(groups):
                sl = group(part, g)
                total = bank[hop, d, slot, sl, :] if hop else jnp.zeros((8, cols), F32)
                for t in range(slots):
                    total = jnp.where(wanted == slots * me + t, tiles[t, sl, :], total)
                bank[hop, d, slot, sl, :] = total
            hop_copy(d, hop + 1, slot, part).start()

    def halo_copies(slot):
        down = remote(pre.at[slot, pl.ds(rows - HALO, HALO)], halo.at[slot, 0],
                      hs.at[slot, 0], hr.at[slot, 0], {"quad": at_quad(1)})
        up = remote(pre.at[slot, pl.ds(0, HALO)], halo.at[slot, 1],
                    hs.at[slot, 1], hr.at[slot, 1], {"quad": at_quad(nq - 1)})
        return down, up

    lane = lax.broadcasted_iota(jnp.int32, (HALO, LANES), 1)

    def spread(x, slot, first):
        shift = lax.rem(cols + taps // 2 - offs[slot], cols)
        x = pltpu.roll(x, shift, 1)
        head = x[:, :LANES]
        ext = jnp.concatenate(
            [jnp.where(lane >= taps // 2, head, 0.0), x[:, LANES:], jnp.where(lane < taps // 2, head, 0.0)],
            axis=1,
        )
        high, low = split(ext)
        width = cols + LANES
        tst[first:first + HALO, :width] = high
        tst[EXT + first:EXT + first + HALO, :width] = high
        tst[2 * EXT + first:2 * EXT + first + HALO, :width] = low

    own_row = lax.broadcasted_iota(jnp.int32, (32, LANES), 0)
    own_col = lax.broadcasted_iota(jnp.int32, (32, LANES), 1)

    def gram_copies(slot):
        return [
            remote(gbuf.at[slot, 0], gbuf.at[slot, step], gs.at[slot, step - 1], gr.at[slot, step - 1],
                   {"quad": at_quad(step)})
            for step in range(1, nq)
        ]

    def assemble(slot):
        for part in range(CHUNKS):
            for d in range(2):
                hop_copy(d, REACH, slot, part).wait_recv()
        wanted = owner(0, slot)
        for g in range(rows // 8):
            sl = pl.ds(g * 8, 8)
            total = bank[REACH, 0, slot, sl, :] + bank[REACH, 1, slot, sl, :]
            for t in range(slots):
                total = jnp.where(wanted == slots * me + t, tiles[t, sl, :], total)
            pre[slot, sl, :] = total
        down, up = halo_copies(slot)

        @pl.when(q < nq - 1)
        def _():
            down.start()

        @pl.when(q > 0)
        def _():
            up.start()

        for g in range(rows // HALO):
            spread(pre[slot, g * HALO:(g + 1) * HALO, :], slot, HALO + g * HALO)

    def edges(slot):
        down, up = halo_copies(slot)

        @pl.when(q > 0)
        def _():
            down.wait_recv()

        @pl.when(q < nq - 1)
        def _():
            up.wait_recv()

        spread(halo[slot, 0], slot, 0)
        spread(halo[slot, 1], slot, HALO + rows)

    def row_step():
        chunk = count * HALO

        @pl.loop(0, (cols + 2 * LANES) // (2 * LANES), unroll=True)
        def _(n):
            sl = pl.ds(pl.multiple_of(n * 2 * LANES, 2 * LANES), 2 * LANES)
            weight = tst[:, sl]
            for piece in range(count * rows // chunk):
                rsl = pl.ds(piece * chunk, chunk)
                high, low = split(jnp.dot(rmat[rsl, :], weight, preferred_element_type=F32))
                yhi[rsl, sl] = high
                ylo[rsl, sl] = low

    bounds = (0, 8, 16, 24, count)

    def column_step(segment):
        @pl.loop(bounds[segment], bounds[segment + 1], unroll=True)
        def _(k):
            rsl = pl.ds(pl.multiple_of(k * rows, 16), rows)
            left = jnp.concatenate(
                [y[rsl, n * LANES:(n + 2) * LANES] for y in (yhi, ylo) for n in range(blocks)], axis=0
            )
            out = jnp.dot(left, bmat[k], preferred_element_type=F32)
            out = out[:, :LANES] + out[:, LANES:]
            out = out[:rows * blocks] + out[rows * blocks:]
            for n in range(blocks):
                img[k, :, n * LANES:(n + 1) * LANES] = out[n * rows:(n + 1) * rows]

    def products(slot):
        img[count] = sci[slot]
        gacc[...] = jnp.zeros_like(gacc)

        @pl.loop(0, rows // 8, unroll=True)
        def _(g):
            x = img[:, pl.ds(pl.multiple_of(g * 8, 8), 8), :].reshape(256, cols)
            high, low = split(x)
            gacc[:, :256] += lax.dot_general(high, high, (((1,), (1,)), ((), ())), preferred_element_type=F32)
            gacc[:, 256:] += lax.dot_general(high, low, (((1,), (1,)), ((), ())), preferred_element_type=F32)

        srow = lax.broadcasted_iota(jnp.int32, (256, 256), 0)
        scol = lax.broadcasted_iota(jnp.int32, (256, 256), 1)
        same = lax.rem(srow, 8) == lax.rem(scol, 8)
        prow = lax.broadcasted_iota(jnp.int32, (256, LANES), 0)
        pcol = lax.broadcasted_iota(jnp.int32, (256, LANES), 1)
        gather = (lax.div(prow, 8) == pcol).astype(F32)

        def reduced(x):
            x = jnp.where(same, x, 0.0).reshape(32, 8, 256).sum(axis=1)
            return jnp.dot(x, gather, precision=HIGHEST, preferred_element_type=F32)

        main = reduced(gacc[:, :256])
        cross = reduced(gacc[:, 256:])
        square = jnp.concatenate([cross, jnp.zeros((96, LANES), F32)], axis=0)
        gbuf[slot, 0] = main + cross + square.T[:32]
        for copy in gram_copies(slot):
            copy.start()

    def solve(slot, middle):
        for copy in gram_copies(slot):
            copy.wait_recv()
        total = gbuf[slot, lax.rem(q + nq, nq)]
        for source in range(1, nq):
            total = total + gbuf[slot, lax.rem(q + nq - source, nq)]
        system = total / pixels + jnp.where((own_row == own_col) & (own_col < count), 0.01, 0.0)
        for j in range(0, count - 1, 2):
            if j == count // 2 - 1:
                middle()
            first_col = jnp.broadcast_to(system[:, j:j + 1], (32, LANES))
            second_col = jnp.broadcast_to(system[:, j + 1:j + 2], (32, LANES))
            first_row, second_row = system[j:j + 1, :], system[j + 1:j + 2, :]
            a, b = first_col[j:j + 1, :], second_col[j:j + 1, :]
            c, d = first_col[j + 1:j + 2, :], second_col[j + 1:j + 2, :]
            inverse = 1.0 / (a * d - b * c)
            first = (d * first_row - b * second_row) * inverse
            second = (a * second_row - c * first_row) * inverse
            rest = system - first_col * first - second_col * second
            system = jnp.where(own_row == j, first, jnp.where(own_row == j + 1, second, rest))
        last = count - 1
        pivot_col = jnp.broadcast_to(system[:, last:last + 1], (32, LANES))
        scaled = system[last:last + 1, :] * (1.0 / pivot_col[last:last + 1, :])
        system = jnp.where(own_row == last, scaled, system - pivot_col * scaled)
        cs[...] = jnp.broadcast_to(system[:, count:count + 1], (32, LANES))

    def spread_copy(d, hop, slot, part):
        source = dt.at[slot, part_rows(part)] if hop == 0 else dbank.at[d, hop - 1, slot, part_rows(part)]
        return remote(source, dbank.at[d, hop, slot, part_rows(part)],
                      ds_.at[d, hop, slot, part], dr.at[d, hop, slot, part], ahead[d])

    def subtract(slot):
        for part in range(CHUNKS):
            for g in range(groups):
                sl = group(part, g)
                total = sci[slot, sl, :]
                for k in range(count):
                    weight = jnp.broadcast_to(cs[k:k + 1, :], (8, LANES))
                    total = total - jnp.concatenate([weight] * blocks, axis=1) * img[k, sl, :]
                diff[slot, sl, :] = total
                dt[slot, sl, :] = pltpu.roll(total, offs[slot], 1)
            for d in range(2):
                spread_copy(d, 0, slot, part).start()

    def forward(hop, slot, part):
        for d in range(2):
            spread_copy(d, hop, slot, part).wait_recv()
            if hop + 1 < REACH:
                spread_copy(d, hop + 1, slot, part).start()

    def add(step, slot, data, parts=range(CHUNKS)):
        wanted = owner(step, slot)
        for part in parts:
            for g in range(groups):
                value = data[group(part, g), :]
                for t in range(slots):
                    coadd[t, group(part, g), :] += jnp.where(wanted == slots * me + t, value, 0.0)

    def nothing():
        pass

    for part in range(CHUNKS):
        relay(0, 0, part)
    bands(0, 16)
    for part in range(CHUNKS):
        relay(1, 0, part)
    relay(0, 1, 0)
    bands(16, 24)
    for part in range(CHUNKS):
        relay(2, 0, part)
    for part in range(1, CHUNKS):
        relay(0, 1, part)
    bands(24, count)
    for t in range(slots):
        coadd[t] = jnp.zeros((rows, cols), F32)

    relay(1, 1, 0)
    assemble(0)
    relay(1, 1, 1)
    edges(0)
    row_step()
    relay(1, 1, 2)
    column_step(0)
    column_step(1)
    relay(2, 1, 0)
    column_step(2)
    relay(2, 1, 1)
    column_step(3)
    products(0)
    relay(2, 1, 2)
    solve(0, nothing)
    subtract(0)
    assemble(1)
    add(0, 0, dt.at[0])

    edges(1)
    row_step()
    column_step(0)
    column_step(1)
    column_step(2)
    forward(0, 0, 0)
    column_step(3)
    forward(0, 0, 1)
    products(1)
    forward(0, 0, 2)
    forward(1, 0, 0)
    forward(1, 0, 1)
    solve(1, functools.partial(forward, 1, 0, 2))
    subtract(1)

    add(0, 1, dt.at[1])
    for d, sign in enumerate(SIGN):
        add(-sign, 0, dbank.at[d, 0, 0])
    for part in range(CHUNKS):
        forward(0, 1, part)
    for d, sign in enumerate(SIGN):
        add(-2 * sign, 0, dbank.at[d, 1, 0])
    for part in range(CHUNKS):
        forward(1, 1, part)
    for part in range(CHUNKS):
        forward(2, 0, part)
    for d, sign in enumerate(SIGN):
        add(-3 * sign, 0, dbank.at[d, 2, 0])
        add(-sign, 1, dbank.at[d, 0, 1])
        add(-2 * sign, 1, dbank.at[d, 1, 1])
    for part in range(CHUNKS):
        forward(2, 1, part)
        for d, sign in enumerate(SIGN):
            add(-3 * sign, 1, dbank.at[d, 2, 1], (part,))

    for slot in range(slots):
        down, up = halo_copies(slot)

        @pl.when(q < nq - 1)
        def _():
            down.wait_send()

        @pl.when(q > 0)
        def _():
            up.wait_send()

        for copy in gram_copies(slot):
            copy.wait_send()
        for part in range(CHUNKS):
            for d in range(2):
                for hop in range(REACH):
                    hop_copy(d, hop + 1, slot, part).wait_send()
                    spread_copy(d, hop, slot, part).wait_send()


def on_device(science, reference_tiles, visit_tiles, offsets, basis_rows, basis_cols):
    slots, rows, cols = science.shape
    count = basis_rows.shape[0]
    nq = lax.axis_size("quad")
    pixels = nq * rows * cols
    pad = ((0, 32 - count), (0, LANES - basis_rows.shape[1]))
    brow = jnp.pad(basis_rows, pad)
    bcol = jnp.pad(basis_cols[:, ::-1], pad)
    vmem = pl.BlockSpec(memory_space=pltpu.VMEM)
    smem = pl.BlockSpec(memory_space=pltpu.SMEM)
    dma = pltpu.SemaphoreType.DMA
    ext_cols = cols + 2 * LANES
    return pl.pallas_call(
        functools.partial(kernel, float(pixels)),
        out_shape=[jax.ShapeDtypeStruct((slots, rows, cols), F32)] * 2,
        in_specs=[vmem, vmem, smem, smem, vmem, vmem],
        out_specs=[vmem, vmem],
        scratch_shapes=[
            pltpu.VMEM((2 * REACH + 1, 8, LANES), jnp.int32),
            pltpu.VMEM((REACH + 1, 2, slots, rows, cols), F32),
            pltpu.VMEM((slots, rows, cols), F32),
            pltpu.VMEM((slots, 2, HALO, cols), F32),
            pltpu.VMEM((256, ext_cols), BF16),
            pltpu.VMEM((count * rows, 256), BF16),
            pltpu.VMEM((3, 32, 256), F32),
            pltpu.VMEM((count, 256, 256), BF16),
            pltpu.VMEM((count * rows, ext_cols), BF16),
            pltpu.VMEM((count * rows, ext_cols), BF16),
            pltpu.VMEM((count + 1, rows, cols), F32),
            pltpu.VMEM((256, 512), F32),
            pltpu.VMEM((slots, nq, 32, LANES), F32),
            pltpu.VMEM((32, LANES), F32),
            pltpu.VMEM((slots, rows, cols), F32),
            pltpu.VMEM((2, REACH, slots, rows, cols), F32),
            dma((2 * REACH + 1,)), dma((2 * REACH + 1,)),
            dma((REACH, 2, slots, CHUNKS)), dma((REACH, 2, slots, CHUNKS)),
            dma((slots, 2)), dma((slots, 2)),
            dma((slots, nq - 1)), dma((slots, nq - 1)),
            dma((2, REACH, slots, CHUNKS)), dma((2, REACH, slots, CHUNKS)),
        ],
        compiler_params=pltpu.CompilerParams(
            collective_id=0, has_side_effects=True, vmem_limit_bytes=56 * 1024 * 1024
        ),
        cost_estimate=pl.CostEstimate(flops=8_000_000_000, bytes_accessed=2_000_000, transcendentals=0),
    )(science, reference_tiles, visit_tiles, offsets, brow, bcol)


def solution(mesh):
    tiles = P("visit", "quad", None)
    return jax.shard_map(
        on_device,
        mesh=mesh,
        in_specs=(tiles, tiles, P("visit", None), P("visit"), P(), P()),
        out_specs=(tiles, tiles),
        check_vma=False,
    )
```

```python
import functools

import jax
import jax.numpy as jnp
from jax import lax
from jax.experimental import pallas as pl
from jax.experimental.pallas import tpu as pltpu
from jax.sharding import PartitionSpec as P

MESH = pl.DeviceIdType.MESH
REACH = 3
LANES = 128
HALO = 16
CHUNKS = 3
EXT = 80
HIGHEST = lax.Precision.HIGHEST
F32 = jnp.float32
BF16 = jnp.bfloat16
SIGN = (1, -1)


def split(x):
    high = x.astype(BF16)
    return high, (x - high.astype(F32)).astype(BF16)


def kernel(
    pixels,
    sci, tiles, pairs, offs, brow, bcol,
    diff, coadd,
    metas, bank, pre, halo, tst, rmat, base, bmat, yhi, ylo, img,
    gacc, gbuf, cs, dt, dbank,
    ms, mr, ts, tr, hs, hr, gs, gr, ds_, dr,
):
    slots, rows, cols = sci.shape
    taps = 31
    count = 31
    chunk_rows = rows // CHUNKS
    nv, nq = lax.axis_size("visit"), lax.axis_size("quad")
    me, q = lax.axis_index("visit"), lax.axis_index("quad")
    blocks = cols // LANES
    groups = chunk_rows // 8

    def at_visit(step):
        return lax.rem(me + step + nv, nv)

    def at_quad(step):
        return lax.rem(q + step, nq)

    def remote(src, dst, send, recv, device):
        return pltpu.make_async_remote_copy(
            src_ref=src, dst_ref=dst, send_sem=send, recv_sem=recv,
            device_id=device, device_id_type=MESH,
        )

    steps = [step * sign for step in range(1, REACH + 1) for sign in SIGN]
    barrier = pltpu.get_barrier_semaphore()
    for step in steps:
        pl.semaphore_signal(barrier, inc=1, device_id={"visit": at_visit(step)}, device_id_type=MESH)
    for step in range(1, nq):
        pl.semaphore_signal(barrier, inc=1, device_id={"quad": at_quad(step)}, device_id_type=MESH)

    line = lax.broadcasted_iota(jnp.int32, (8, LANES), 0)
    own = jnp.zeros((8, LANES), jnp.int32)
    for slot in range(slots):
        for place, value in enumerate((pairs[slot, 0], pairs[slot, 1], offs[slot])):
            own = jnp.where(line == 3 * slot + place, value, own)
    metas[REACH] = own
    pl.semaphore_wait(barrier, len(steps) + nq - 1)

    meta_copies = [
        remote(metas.at[REACH], metas.at[REACH - step], ms.at[REACH - step], mr.at[REACH - step],
               {"visit": at_visit(step)})
        for step in steps
    ]
    for copy in meta_copies:
        copy.start()
    ahead = [{"visit": at_visit(sign)} for sign in SIGN]
    tst[...] = jnp.zeros_like(tst)
    bmat[...] = jnp.zeros_like(bmat)
    blank = jnp.zeros((32, LANES), F32)
    row_high = brow[...].astype(BF16).astype(F32)
    row_low = brow[...] - row_high
    wide_high = jnp.concatenate([row_high, blank], axis=1)
    wide_low = jnp.concatenate([row_low, blank], axis=1)
    base[0] = (
        pltpu.roll(wide_high, 1, 1) + pltpu.roll(wide_low, EXT + 1, 1) + pltpu.roll(wide_high, 2 * EXT + 1, 1)
    )
    col_high = bcol[...].astype(BF16).astype(F32)
    back = 2 * LANES - (taps - 1)
    base[1] = pltpu.roll(jnp.concatenate([col_high, blank], axis=1), back, 1)
    base[2] = pltpu.roll(jnp.concatenate([bcol[...] - col_high, blank], axis=1), back, 1)

    @pl.loop(0, count)
    def _(k):
        first = pl.multiple_of(k * rows, 16)
        line_k = jnp.broadcast_to(base[0, pl.ds(k, 1), :], (rows, 2 * LANES))
        rmat[pl.ds(first, rows), :] = pltpu.roll(line_k, 0, 1, stride=1, stride_axis=0).astype(BF16)

    def bands(first, last):
        @pl.loop(first, last)
        def _(k):
            for part in range(2):
                line_k = jnp.broadcast_to(base[1 + part, pl.ds(k, 1), :], (EXT, 2 * LANES))
                band = pltpu.roll(line_k, 0, 1, stride=1, stride_axis=0)
                for piece in range(2):
                    if piece:
                        band = pltpu.roll(band, EXT, 1)
                    bmat[k, piece * EXT:(piece + 1) * EXT, part * LANES:(part + 1) * LANES] = (
                        band[:, :LANES].astype(BF16)
                    )

    @pl.when(q == 0)
    def _():
        for slot in range(slots):
            halo[slot, 0] = jnp.zeros((HALO, cols), F32)

    @pl.when(q == nq - 1)
    def _():
        for slot in range(slots):
            halo[slot, 1] = jnp.zeros((HALO, cols), F32)

    for copy in meta_copies:
        copy.wait()

    column = lax.broadcasted_iota(jnp.int32, (8, cols), 1)

    def owner(step, slot):
        def wide(place):
            value = metas[REACH + step, 3 * slot + place:3 * slot + place + 1, :]
            return jnp.concatenate([jnp.broadcast_to(value, (8, LANES))] * blocks, axis=1)
        return jnp.where(column >= wide(2), wide(0), wide(1))

    def group(part, g):
        return pl.ds(part * chunk_rows + g * 8, 8)

    def part_rows(part):
        return pl.ds(part * chunk_rows, chunk_rows)

    def hop_copy(d, hop, slot, part):
        return remote(bank.at[hop - 1, d, slot, part_rows(part)], bank.at[hop, d, slot, part_rows(part)],
                      ts.at[hop - 1, d, slot, part], tr.at[hop - 1, d, slot, part], ahead[d])

    def relay(hop, slot, part):
        for d, sign in enumerate(SIGN):
            wanted = owner((REACH - hop) * sign, slot)
            if hop:
                hop_copy(d, hop, slot, part).wait_recv()
            for g in range(groups):
                sl = group(part, g)
                total = bank[hop, d, slot, sl, :] if hop else jnp.zeros((8, cols), F32)
                for t in range(slots):
                    total = jnp.where(wanted == slots * me + t, tiles[t, sl, :], total)
                bank[hop, d, slot, sl, :] = total
            hop_copy(d, hop + 1, slot, part).start()

    def halo_copies(slot):
        down = remote(pre.at[slot, pl.ds(rows - HALO, HALO)], halo.at[slot, 0],
                      hs.at[slot, 0], hr.at[slot, 0], {"quad": at_quad(1)})
        up = remote(pre.at[slot, pl.ds(0, HALO)], halo.at[slot, 1],
                    hs.at[slot, 1], hr.at[slot, 1], {"quad": at_quad(nq - 1)})
        return down, up

    lane = lax.broadcasted_iota(jnp.int32, (HALO, LANES), 1)

    def spread(x, slot, first):
        shift = lax.rem(cols + taps // 2 - offs[slot], cols)
        x = pltpu.roll(x, shift, 1)
        head = x[:, :LANES]
        ext = jnp.concatenate(
            [jnp.where(lane >= taps // 2, head, 0.0), x[:, LANES:], jnp.where(lane < taps // 2, head, 0.0)],
            axis=1,
        )
        high, low = split(ext)
        width = cols + LANES
        tst[first:first + HALO, :width] = high
        tst[EXT + first:EXT + first + HALO, :width] = high
        tst[2 * EXT + first:2 * EXT + first + HALO, :width] = low

    own_row = lax.broadcasted_iota(jnp.int32, (32, LANES), 0)
    own_col = lax.broadcasted_iota(jnp.int32, (32, LANES), 1)

    def gram_copies(slot):
        return [
            remote(gbuf.at[slot, 0], gbuf.at[slot, step], gs.at[slot, step - 1], gr.at[slot, step - 1],
                   {"quad": at_quad(step)})
            for step in range(1, nq)
        ]

    def assemble(slot):
        for part in range(CHUNKS):
            for d in range(2):
                hop_copy(d, REACH, slot, part).wait_recv()
        wanted = owner(0, slot)
        for g in range(rows // 8):
            sl = pl.ds(g * 8, 8)
            total = bank[REACH, 0, slot, sl, :] + bank[REACH, 1, slot, sl, :]
            for t in range(slots):
                total = jnp.where(wanted == slots * me + t, tiles[t, sl, :], total)
            pre[slot, sl, :] = total
        down, up = halo_copies(slot)

        @pl.when(q < nq - 1)
        def _():
            down.start()

        @pl.when(q > 0)
        def _():
            up.start()

        for g in range(rows // HALO):
            spread(pre[slot, g * HALO:(g + 1) * HALO, :], slot, HALO + g * HALO)

    def edges(slot):
        down, up = halo_copies(slot)

        @pl.when(q > 0)
        def _():
            down.wait_recv()

        @pl.when(q < nq - 1)
        def _():
            up.wait_recv()

        spread(halo[slot, 0], slot, 0)
        spread(halo[slot, 1], slot, HALO + rows)

    def row_step():
        chunk = count * HALO

        @pl.loop(0, (cols + 2 * LANES) // (2 * LANES), unroll=True)
        def _(n):
            sl = pl.ds(pl.multiple_of(n * 2 * LANES, 2 * LANES), 2 * LANES)
            weight = tst[:, sl]
            for piece in range(count * rows // chunk):
                rsl = pl.ds(piece * chunk, chunk)
                high, low = split(jnp.dot(rmat[rsl, :], weight, preferred_element_type=F32))
                yhi[rsl, sl] = high
                ylo[rsl, sl] = low

    bounds = (0, 8, 16, 24, count)

    def column_step(segment):
        @pl.loop(bounds[segment], bounds[segment + 1], unroll=True)
        def _(k):
            rsl = pl.ds(pl.multiple_of(k * rows, 16), rows)
            left = jnp.concatenate(
                [y[rsl, n * LANES:(n + 2) * LANES] for y in (yhi, ylo) for n in range(blocks)], axis=0
            )
            out = jnp.dot(left, bmat[k], preferred_element_type=F32)
            out = out[:, :LANES] + out[:, LANES:]
            out = out[:rows * blocks] + out[rows * blocks:]
            for n in range(blocks):
                img[k, :, n * LANES:(n + 1) * LANES] = out[n * rows:(n + 1) * rows]

    def products(slot):
        img[count] = sci[slot]
        gacc[...] = jnp.zeros_like(gacc)

        @pl.loop(0, rows // 8, unroll=True)
        def _(g):
            x = img[:, pl.ds(pl.multiple_of(g * 8, 8), 8), :].reshape(256, cols)
            high, low = split(x)
            gacc[:, :256] += lax.dot_general(high, high, (((1,), (1,)), ((), ())), preferred_element_type=F32)
            gacc[:, 256:] += lax.dot_general(high, low, (((1,), (1,)), ((), ())), preferred_element_type=F32)

        srow = lax.broadcasted_iota(jnp.int32, (256, 256), 0)
        scol = lax.broadcasted_iota(jnp.int32, (256, 256), 1)
        same = lax.rem(srow, 8) == lax.rem(scol, 8)
        prow = lax.broadcasted_iota(jnp.int32, (256, LANES), 0)
        pcol = lax.broadcasted_iota(jnp.int32, (256, LANES), 1)
        gather = (lax.div(prow, 8) == pcol).astype(F32)

        def reduced(x):
            x = jnp.where(same, x, 0.0).reshape(32, 8, 256).sum(axis=1)
            return jnp.dot(x, gather, precision=HIGHEST, preferred_element_type=F32)

        main = reduced(gacc[:, :256])
        cross = reduced(gacc[:, 256:])
        square = jnp.concatenate([cross, jnp.zeros((96, LANES), F32)], axis=0)
        gbuf[slot, 0] = main + cross + square.T[:32]
        for copy in gram_copies(slot):
            copy.start()

    def solve(slot, middle):
        for copy in gram_copies(slot):
            copy.wait_recv()
        total = gbuf[slot, lax.rem(q + nq, nq)]
        for source in range(1, nq):
            total = total + gbuf[slot, lax.rem(q + nq - source, nq)]
        system = total / pixels + jnp.where((own_row == own_col) & (own_col < count), 0.01, 0.0)
        for j in range(0, count - 1, 2):
            if j == count // 2 - 1:
                middle()
            first_col = jnp.broadcast_to(system[:, j:j + 1], (32, LANES))
            second_col = jnp.broadcast_to(system[:, j + 1:j + 2], (32, LANES))
            first_row, second_row = system[j:j + 1, :], system[j + 1:j + 2, :]
            a, b = first_col[j:j + 1, :], second_col[j:j + 1, :]
            c, d = first_col[j + 1:j + 2, :], second_col[j + 1:j + 2, :]
            inverse = 1.0 / (a * d - b * c)
            first = (d * first_row - b * second_row) * inverse
            second = (a * second_row - c * first_row) * inverse
            rest = system - first_col * first - second_col * second
            system = jnp.where(own_row == j, first, jnp.where(own_row == j + 1, second, rest))
        last = count - 1
        pivot_col = jnp.broadcast_to(system[:, last:last + 1], (32, LANES))
        scaled = system[last:last + 1, :] * (1.0 / pivot_col[last:last + 1, :])
        system = jnp.where(own_row == last, scaled, system - pivot_col * scaled)
        cs[...] = jnp.broadcast_to(system[:, count:count + 1], (32, LANES))

    def spread_copy(d, hop, slot, part):
        source = dt.at[slot, part_rows(part)] if hop == 0 else dbank.at[d, hop - 1, slot, part_rows(part)]
        return remote(source, dbank.at[d, hop, slot, part_rows(part)],
                      ds_.at[d, hop, slot, part], dr.at[d, hop, slot, part], ahead[d])

    def subtract(slot):
        for part in range(CHUNKS):
            for g in range(groups):
                sl = group(part, g)
                total = sci[slot, sl, :]
                for k in range(count):
                    weight = jnp.broadcast_to(cs[k:k + 1, :], (8, LANES))
                    total = total - jnp.concatenate([weight] * blocks, axis=1) * img[k, sl, :]
                diff[slot, sl, :] = total
                dt[slot, sl, :] = pltpu.roll(total, offs[slot], 1)
            for d in range(2):
                spread_copy(d, 0, slot, part).start()

    def forward(hop, slot, part):
        for d in range(2):
            spread_copy(d, hop, slot, part).wait_recv()
            if hop + 1 < REACH:
                spread_copy(d, hop + 1, slot, part).start()

    def add(step, slot, data, parts=range(CHUNKS)):
        wanted = owner(step, slot)
        for part in parts:
            for g in range(groups):
                value = data[group(part, g), :]
                for t in range(slots):
                    coadd[t, group(part, g), :] += jnp.where(wanted == slots * me + t, value, 0.0)

    def nothing():
        pass

    for part in range(CHUNKS):
        relay(0, 0, part)
    bands(0, 16)
    for part in range(CHUNKS):
        relay(1, 0, part)
    bands(16, 24)
    for part in range(CHUNKS):
        relay(2, 0, part)
    for part in range(CHUNKS):
        relay(0, 1, part)
    bands(24, count)
    for t in range(slots):
        coadd[t] = jnp.zeros((rows, cols), F32)

    assemble(0)
    relay(1, 1, 0)
    edges(0)
    relay(1, 1, 1)
    row_step()
    column_step(0)
    relay(1, 1, 2)
    column_step(1)
    column_step(2)
    relay(2, 1, 0)
    column_step(3)
    relay(2, 1, 1)
    products(0)
    relay(2, 1, 2)
    solve(0, nothing)
    subtract(0)
    assemble(1)
    add(0, 0, dt.at[0])

    edges(1)
    row_step()
    column_step(0)
    column_step(1)
    column_step(2)
    forward(0, 0, 0)
    column_step(3)
    forward(0, 0, 1)
    products(1)
    forward(0, 0, 2)
    forward(1, 0, 0)
    forward(1, 0, 1)
    solve(1, functools.partial(forward, 1, 0, 2))
    subtract(1)

    add(0, 1, dt.at[1])
    for d, sign in enumerate(SIGN):
        add(-sign, 0, dbank.at[d, 0, 0])
    for part in range(CHUNKS):
        forward(0, 1, part)
    for d, sign in enumerate(SIGN):
        add(-2 * sign, 0, dbank.at[d, 1, 0])
    for part in range(CHUNKS):
        forward(1, 1, part)
    for part in range(CHUNKS):
        forward(2, 0, part)
    for d, sign in enumerate(SIGN):
        add(-3 * sign, 0, dbank.at[d, 2, 0])
        add(-sign, 1, dbank.at[d, 0, 1])
        add(-2 * sign, 1, dbank.at[d, 1, 1])
    for part in range(CHUNKS):
        forward(2, 1, part)
        for d, sign in enumerate(SIGN):
            add(-3 * sign, 1, dbank.at[d, 2, 1], (part,))

    for slot in range(slots):
        down, up = halo_copies(slot)

        @pl.when(q < nq - 1)
        def _():
            down.wait_send()

        @pl.when(q > 0)
        def _():
            up.wait_send()

        for copy in gram_copies(slot):
            copy.wait_send()
        for part in range(CHUNKS):
            for d in range(2):
                for hop in range(REACH):
                    hop_copy(d, hop + 1, slot, part).wait_send()
                    spread_copy(d, hop, slot, part).wait_send()


def on_device(science, reference_tiles, visit_tiles, offsets, basis_rows, basis_cols):
    slots, rows, cols = science.shape
    count = basis_rows.shape[0]
    nq = lax.axis_size("quad")
    pixels = nq * rows * cols
    pad = ((0, 32 - count), (0, LANES - basis_rows.shape[1]))
    brow = jnp.pad(basis_rows, pad)
    bcol = jnp.pad(basis_cols[:, ::-1], pad)
    vmem = pl.BlockSpec(memory_space=pltpu.VMEM)
    smem = pl.BlockSpec(memory_space=pltpu.SMEM)
    dma = pltpu.SemaphoreType.DMA
    ext_cols = cols + 2 * LANES
    return pl.pallas_call(
        functools.partial(kernel, float(pixels)),
        out_shape=[jax.ShapeDtypeStruct((slots, rows, cols), F32)] * 2,
        in_specs=[vmem, vmem, smem, smem, vmem, vmem],
        out_specs=[vmem, vmem],
        scratch_shapes=[
            pltpu.VMEM((2 * REACH + 1, 8, LANES), jnp.int32),
            pltpu.VMEM((REACH + 1, 2, slots, rows, cols), F32),
            pltpu.VMEM((slots, rows, cols), F32),
            pltpu.VMEM((slots, 2, HALO, cols), F32),
            pltpu.VMEM((256, ext_cols), BF16),
            pltpu.VMEM((count * rows, 256), BF16),
            pltpu.VMEM((3, 32, 256), F32),
            pltpu.VMEM((count, 256, 256), BF16),
            pltpu.VMEM((count * rows, ext_cols), BF16),
            pltpu.VMEM((count * rows, ext_cols), BF16),
            pltpu.VMEM((count + 1, rows, cols), F32),
            pltpu.VMEM((256, 512), F32),
            pltpu.VMEM((slots, nq, 32, LANES), F32),
            pltpu.VMEM((32, LANES), F32),
            pltpu.VMEM((slots, rows, cols), F32),
            pltpu.VMEM((2, REACH, slots, rows, cols), F32),
            dma((2 * REACH + 1,)), dma((2 * REACH + 1,)),
            dma((REACH, 2, slots, CHUNKS)), dma((REACH, 2, slots, CHUNKS)),
            dma((slots, 2)), dma((slots, 2)),
            dma((slots, nq - 1)), dma((slots, nq - 1)),
            dma((2, REACH, slots, CHUNKS)), dma((2, REACH, slots, CHUNKS)),
        ],
        compiler_params=pltpu.CompilerParams(
            collective_id=0, has_side_effects=True, vmem_limit_bytes=56 * 1024 * 1024
        ),
        cost_estimate=pl.CostEstimate(flops=8_000_000_000, bytes_accessed=2_000_000, transcendentals=0),
    )(science, reference_tiles, visit_tiles, offsets, brow, bcol)


def solution(mesh):
    tiles = P("visit", "quad", None)
    return jax.shard_map(
        on_device,
        mesh=mesh,
        in_specs=(tiles, tiles, P("visit", None), P("visit"), P(), P()),
        out_specs=(tiles, tiles),
        check_vma=False,
    )
```
